256 devices in a mesh: section: 8 (over z_lo, core), expert: 8 (over x, z_hi), edata: 4 (over y).
Axes of the slice: x: 4, y: 4, z: 8 (z_hi: 2, z_lo: 4; z = z_hi * 4 + z_lo), core: 2. Of those that a mesh axis runs over, the one named last changes fastest.
Arguments:
- normed_input: bfloat16 [4096, 4096], P(('expert', 'edata'), 'section'), may hold values from -6 to 6
- output_grad: bfloat16 [4096, 4096], P(('expert', 'edata'), 'section'), may hold values from -6 to 6
- expert_ids: int32 [4096, 2], P(('expert', 'edata')), may hold values from 0 to 7, as said below
- slot_pos: int32 [4096, 2], P(('expert', 'edata')), may hold values from 0 to 32, as said below
- router_weight: bfloat16 [4096, 8], replicated, may hold values from -0.09375 to 0.09375
- gate_weight: bfloat16 [8, 7168, 4096], P('expert', ('section', 'edata')), may hold values from -0.09375 to 0.09375
- up_weight: bfloat16 [8, 7168, 4096], P('expert', ('section', 'edata')), may hold values from -0.09375 to 0.09375
- down_weight: bfloat16 [8, 7168, 4096], P('expert', ('section', 'edata')), may hold values from -0.0625 to 0.0625
- saved_gate: bfloat16 [8, 7168, 1024], P('expert', ('section', 'edata')), may hold values from -6 to 6
- saved_up: bfloat16 [8, 7168, 1024], P('expert', ('section', 'edata')), may hold values from -30 to 30
Outputs:
- input_grad: bfloat16 [4096, 4096], P(('expert', 'edata'), 'section')
- grad_router: float32 [4096, 8], P(('section', 'expert', 'edata'))
- grad_gate: bfloat16 [8, 7168, 4096], P('expert', ('section', 'edata'))
- grad_up: bfloat16 [8, 7168, 4096], P('expert', ('section', 'edata'))
- grad_down: bfloat16 [8, 7168, 4096], P('expert', ('section', 'edata'))
The draws below stay inside these ranges and needn't reach their ends.
Inputs may be any that keep to these rules, and one draw needn't show every extreme that they name: `expert_ids`: the two ids of a token differ. `slot_pos`: within each aligned block of 128 tokens (the tokens of one device), the assignments naming one expert hold distinct positions 0, 1, 2 and so on, in an order drawn for each block; an assignment at position 32 or beyond is dropped and holds 32. In every block some expert fills all 32 positions.
All inputs are finite; a program needn't handle non-finite values.
Results may differ from the reference program's by a relative error of at most 0.02.
Values may be sent and summed in bfloat16 or wider, within the bound.
No kernel may reach another device: no remote copies, remote signals or barrier semaphores. Data moves between devices by JAX's collectives and lax.ppermute only.
A program may use at most 128 MiB of HBM per device.

```python
import math
import jax
import jax.numpy as jnp
from jax import lax

D = 4096
FF_DEV = 224
TOK_DEV = 128
EXPERTS = 8
FFW = 7168
CAP = 32
SLOTS = 1024
TOKENS = 4096
N_SECTION = 8
N_EDATA = 4


def routing_table(key):
    blocks = TOKENS // TOK_DEV
    key_pop, key_pick, key_step, key_order = jax.random.split(key, 4)
    popular = jax.random.randint(key_pop, (), 0, EXPERTS)
    pick_draw = jax.random.randint(key_pick, (TOKENS,), 0, 2 * EXPERTS)
    first_id = jnp.where(pick_draw < EXPERTS, popular, pick_draw - EXPERTS)
    step_id = jax.random.randint(key_step, (TOKENS,), 1, EXPERTS)
    second = (first_id + step_id) % EXPERTS
    chosen = jnp.stack([first_id, second], axis=1).astype(jnp.int32)
    flat_ids = chosen.reshape(blocks, TOK_DEV * 2)
    order_keys = jax.random.split(key_order, blocks)
    priority = jax.vmap(lambda one_key: jax.random.permutation(one_key, TOK_DEV * 2))(order_keys).astype(jnp.int32)
    same_expert = flat_ids[:, :, None] == flat_ids[:, None, :]
    earlier = priority[:, None, :] < priority[:, :, None]
    position = jnp.sum((same_expert & earlier).astype(jnp.int32), axis=2)
    position = jnp.minimum(position, CAP).reshape(TOKENS, 2).astype(jnp.int32)
    return (chosen, position)


def draw_expert_ids(key, part):
    chosen, position = routing_table(key)
    return chosen


def draw_slot_pos(key, part):
    chosen, position = routing_table(key)
    return position


def draw_saved_up(key, part):
    key = jax.random.fold_in(key, 7)
    key_rough, key_base = jax.random.split(key)
    ramp_scale = jnp.exp(math.log(3.0) * jnp.arange(FFW, dtype=jnp.float32) / FFW)
    rough_scale = jnp.exp(jax.random.uniform(key_rough, (EXPERTS, FFW, 1), jnp.float32, -0.8, 0.8))
    base_draw = jax.random.truncated_normal(key_base, -4.0, 4.0, (EXPERTS, FFW, SLOTS), jnp.float32)
    return (base_draw * ramp_scale[None, :, None] * rough_scale).astype(jnp.bfloat16)


def steps_of(own_key, dims, shards, least, high):
    factor_of, own = 1.0, jax.random.fold_in(own_key, 6)
    for dim, parts in shards:
        heights = jnp.exp(jax.random.uniform(jax.random.fold_in(own, dim), (parts,), jnp.float32, least / len(shards), high / len(shards)))
        factor_of = factor_of * jnp.repeat(heights, dims[dim] // parts).reshape([-1 if axis == dim else 1 for axis in range(len(dims))])
    return factor_of


def noise(key, dims, scale, bound, shards=(), kind=jnp.bfloat16):
    drawn = scale * jax.random.normal(key, dims, jnp.float32)
    if shards:
        drawn = drawn * steps_of(key, dims, shards, -0.22, 0.18)
    return jnp.clip(drawn, -bound, bound).astype(kind)


def setup_inputs(seed: int = 0) -> dict:
    keys = jax.random.split(jax.random.key(seed), 11)
    normed_input = noise(keys[0], (TOKENS, D), 1.0, 6.0, ((0, 32), (1, 8)))
    output_grad = noise(keys[1], (TOKENS, D), 1.0, 6.0, ((0, 32), (1, 8)))
    expert_ids = draw_expert_ids(jax.random.fold_in(keys[10], 71), 0)
    slot_pos = draw_slot_pos(jax.random.fold_in(keys[10], 71), 0)
    router_weight = noise(keys[4], (D, EXPERTS), D ** -0.5, 0.09375)
    gate_weight = noise(keys[5], (EXPERTS, FFW, D), D ** -0.5, 0.09375, ((0, 8), (1, 32)))
    up_weight = noise(keys[6], (EXPERTS, FFW, D), D ** -0.5, 0.09375, ((0, 8), (1, 32)))
    down_weight = noise(keys[7], (EXPERTS, FFW, D), FFW ** -0.5, 0.0625, ((0, 8), (1, 32)))
    saved_gate = noise(keys[8], (EXPERTS, FFW, SLOTS), 1.5, 6.0, ((0, 8), (1, 32)))
    saved_up = draw_saved_up(jax.random.fold_in(keys[10], 71), 0)
    return {"normed_input": normed_input, "output_grad": output_grad, "expert_ids": expert_ids, "slot_pos": slot_pos, "router_weight": router_weight, "gate_weight": gate_weight, "up_weight": up_weight, "down_weight": down_weight, "saved_gate": saved_gate, "saved_up": saved_up}


def silu_parts(pre_value):
    sigmoid_value = jax.nn.sigmoid(pre_value)
    return (pre_value * sigmoid_value, sigmoid_value * (1.0 + pre_value * (1.0 - sigmoid_value)))

def expert_backward(packed):
    rows_x, rows_dy, rows_gate, w_gate, w_up, w_down, pre_gate, pre_up = packed
    gate_rows = rows_gate.astype(jnp.float32)
    pull_back = lax.dot_general(w_down, rows_dy, (((1,), (1,)), ((), ())), preferred_element_type=jnp.float32)
    pre_gate = pre_gate.astype(jnp.float32)
    pre_up = pre_up.astype(jnp.float32)
    activated, derivative = silu_parts(pre_gate)
    hidden = (activated * pre_up).astype(jnp.bfloat16)
    slot_score = lax.optimization_barrier(jnp.sum(hidden.astype(jnp.float32) * pull_back, axis=0))
    back_hidden = gate_rows[None, :] * pull_back
    scaled_dy = (gate_rows[:, None] * rows_dy.astype(jnp.float32)).astype(jnp.bfloat16)
    d_gate = (back_hidden * pre_up * derivative).astype(jnp.bfloat16)
    d_up = (back_hidden * activated).astype(jnp.bfloat16)
    raw_down = jnp.dot(hidden, scaled_dy, preferred_element_type=jnp.float32)
    raw_gate = jnp.dot(d_gate, rows_x, preferred_element_type=jnp.float32)
    raw_up = jnp.dot(d_up, rows_x, preferred_element_type=jnp.float32)
    slab_count = N_SECTION * N_EDATA
    slab_parts = (d_gate.reshape(slab_count, FF_DEV, SLOTS), d_up.reshape(slab_count, FF_DEV, SLOTS), w_gate.reshape(slab_count, FF_DEV, D), w_up.reshape(slab_count, FF_DEV, D))

    def add_slab(running, part):
        slab_gate, slab_up, weight_gate, weight_up = part
        slab_term = jnp.dot(slab_gate.T, weight_gate, preferred_element_type=jnp.float32)
        slab_term = slab_term + jnp.dot(slab_up.T, weight_up, preferred_element_type=jnp.float32)
        rounded = lax.optimization_barrier(slab_term.astype(jnp.bfloat16))
        return (running + rounded.astype(jnp.float32), None)
    slot_dx, _ = lax.scan(add_slab, jnp.zeros((SLOTS, D), jnp.float32), slab_parts)
    return (raw_gate, raw_up, raw_down, slot_dx, slot_score)

def reference(normed_input, output_grad, expert_ids, slot_pos, router_weight, gate_weight, up_weight, down_weight, saved_gate, saved_up):
    logits = jnp.dot(normed_input, router_weight, preferred_element_type=jnp.float32)
    chosen = jnp.take_along_axis(logits, expert_ids, axis=1)
    first_share = jax.nn.sigmoid(chosen[:, 0] - chosen[:, 1])
    gate_share = jnp.stack([first_share, 1.0 - first_share], axis=1).astype(jnp.bfloat16)
    source = (jnp.arange(TOKENS, dtype=jnp.int32) // TOK_DEV)[:, None]
    live_mask = slot_pos < CAP
    target = jnp.where(live_mask, source * CAP + slot_pos, SLOTS).astype(jnp.int32)
    spread_x = jnp.broadcast_to(normed_input[:, None, :], (TOKENS, 2, D))
    spread_dy = jnp.broadcast_to(output_grad[:, None, :], (TOKENS, 2, D))
    rows_x = jnp.zeros((EXPERTS, SLOTS, D), jnp.bfloat16).at[expert_ids, target].set(spread_x, mode='drop')
    rows_dy = jnp.zeros((EXPERTS, SLOTS, D), jnp.bfloat16).at[expert_ids, target].set(spread_dy, mode='drop')
    rows_gate = jnp.zeros((EXPERTS, SLOTS), jnp.bfloat16).at[expert_ids, target].set(gate_share, mode='drop')
    raw_gate, raw_up, raw_down, slot_dx, slot_score = lax.map(expert_backward, (rows_x, rows_dy, rows_gate, gate_weight, up_weight, down_weight, saved_gate, saved_up))
    safe_slot = jnp.minimum(target, SLOTS - 1).astype(jnp.int32)
    picked = slot_dx[expert_ids, safe_slot]
    token_dx = lax.optimization_barrier(jnp.sum(jnp.where(live_mask[:, :, None], picked, 0.0), axis=1))
    gate_grad = jnp.where(live_mask, slot_score[expert_ids, safe_slot], 0.0)
    logit_step = (gate_grad[:, 0] - gate_grad[:, 1]) * first_share * (1.0 - first_share)
    columns = jnp.arange(EXPERTS, dtype=jnp.int32)[None, :]
    logit_grad = jnp.where(columns == expert_ids[:, 0:1], logit_step[:, None], 0.0)
    logit_grad = logit_grad - jnp.where(columns == expert_ids[:, 1:2], logit_step[:, None], 0.0)
    router_float = router_weight.astype(jnp.float32)
    input_grad = (token_dx + jnp.dot(logit_grad, router_float.T, precision=lax.Precision.HIGHEST)).astype(jnp.bfloat16)
    raw_router = jnp.dot(normed_input.astype(jnp.float32).T, logit_grad, precision=lax.Precision.HIGHEST)
    square_sum = jnp.sum(raw_gate * raw_gate) + jnp.sum(raw_up * raw_up) + jnp.sum(raw_down * raw_down)
    square_sum = square_sum + jnp.sum(raw_router * raw_router)
    entry_count = 3.0 * EXPERTS * FFW * D + 1.0 * D * EXPERTS
    factor = 1.0 / jnp.maximum(jnp.sqrt(square_sum / entry_count), 1.0)
    grad_router = factor * raw_router
    grad_gate = (factor * raw_gate).astype(jnp.bfloat16)
    grad_up = (factor * raw_up).astype(jnp.bfloat16)
    grad_down = (factor * raw_down).astype(jnp.bfloat16)
    return (input_grad, grad_router, grad_gate, grad_up, grad_down)
```

```python
import jax
import jax.numpy as jnp
from jax import lax
from jax.sharding import Mesh, PartitionSpec as P

F32 = jnp.float32
BF16 = jnp.bfloat16
RING = 4


def turn(value, axis, step):
    return lax.ppermute(value, axis, [(i, (i + step) % RING) for i in range(RING)])


def swap(value, axis):
    return lax.ppermute(value, axis, [(0, 1), (1, 0)])


def sum_ring(value, axis):
    one, two, three = turn(value, axis, 1), turn(value, axis, 2), turn(value, axis, 3)
    return (value + two) + (one + three)


def sum_pair(value, axis):
    return value + swap(value, axis)


def exchange(rows, sign):
    count = rows.shape[0] // 8
    parts = []
    for j in range(8):
        part = rows[j * count : (j + 1) * count]
        a, b = j // 2, j % 2
        if j:
            pairs = [
                (x * 2 + h, ((x + sign * a) % RING) * 2 + (h ^ b)) for x in range(RING) for h in range(2)
            ]
            part = lax.ppermute(part, ("x", "h"), pairs)
        parts.append(part)
    return jnp.concatenate(parts, axis=0)


def exchange_small(rows, sign):
    parts = rows.reshape(RING, 2, -1)
    near, far = parts[:, 0], swap(parts[:, 1], "h")
    both = jnp.stack([near, far], axis=1)
    out = [both[0]] + [turn(both[a], "x", sign * a) for a in range(1, RING)]
    return jnp.stack(out, axis=0).reshape(rows.shape)


def after(value, *others):
    return lax.optimization_barrier((value,) + others)[0]


def local(
    normed_input,
    output_grad,
    expert_ids,
    slot_pos,
    router_weight,
    gate_weight,
    up_weight,
    down_weight,
    saved_gate,
    saved_up,
):
    z, c, x, h, y = (lax.axis_index(name) for name in ("z", "c", "x", "h", "y"))
    width, experts = router_weight.shape
    tokens, features = normed_input.shape
    hidden_dev = gate_weight.shape[1]
    slot_total = saved_gate.shape[2]
    capacity = slot_total // (8 * RING)
    block = 8 * capacity
    half = RING * features

    near_expert = ((expert_ids // 2 - x) % RING) * 2 + (expert_ids % 2 + h) % 2
    live_mask = slot_pos < capacity
    address = near_expert * capacity + slot_pos
    table = jnp.arange(block, dtype=jnp.int32)[None, :]
    first_pick = (address[:, 0:1] == table) & live_mask[:, 0:1]
    second_pick = (address[:, 1:2] == table) & live_mask[:, 1:2]
    pick_matrix = (first_pick | second_pick).astype(BF16)

    def place(matrix, values):
        return lax.dot_general(
            matrix, values, (((0,), (0,)), ((), ())), preferred_element_type=F32
        ).astype(BF16)

    def gather_z(rows):
        return jnp.concatenate([rows] + [turn(rows, "z", r) for r in range(1, RING)], axis=1)

    dy_rows = gather_z(exchange(place(pick_matrix, output_grad), 1))

    router_rows = lax.dynamic_slice_in_dim(router_weight, (z * 2 + c) * features, features, 0)
    logits = jnp.dot(normed_input, router_rows, preferred_element_type=F32)
    logits = sum_ring(sum_pair(logits, "c"), "z")
    columns = jnp.arange(experts, dtype=jnp.int32)[None, :]
    first_hot = (columns == expert_ids[:, 0:1]).astype(F32)
    second_hot = (columns == expert_ids[:, 1:2]).astype(F32)
    pair_hot = first_hot - second_hot
    first_share = jax.nn.sigmoid(
        jnp.sum(logits * first_hot, axis=1) - jnp.sum(logits * second_hot, axis=1)
    )
    gate_first = first_share.astype(BF16).astype(F32)
    gate_second = (1.0 - first_share).astype(BF16).astype(F32)
    gate_matrix = jnp.where(first_pick, gate_first[:, None], 0.0) + jnp.where(
        second_pick, gate_second[:, None], 0.0
    )
    slot_gate = exchange_small(jnp.sum(gate_matrix, axis=0), 1)
    gate_rows = [slot_gate] + [turn(slot_gate, "y", -k) for k in range(1, RING)]
    x_rows = exchange(place(gate_matrix.astype(BF16), normed_input), 1)

    order = jnp.arange(slot_total, dtype=jnp.int32)
    from_y = (y + order // block) % RING
    from_x = (x - (order % block) // (2 * capacity)) % RING
    from_h = (h + (order // capacity) % 2) % 2
    source = ((from_x * 2 + from_h) * RING + from_y) * capacity + order % capacity
    shuffle = (order[:, None] == source[None, :]).astype(BF16)
    pre_gate = jnp.dot(saved_gate[0], shuffle, preferred_element_type=F32)
    pre_up = jnp.dot(saved_up[0], shuffle, preferred_element_type=F32)
    sigmoid_gate = jax.nn.sigmoid(pre_gate)
    activated = pre_gate * sigmoid_gate
    hidden = (activated * pre_up).astype(BF16)
    gate_slope = pre_up * sigmoid_gate * (1.0 + pre_gate * (1.0 - sigmoid_gate))

    def sections(d):
        return [((z - r) % RING) * 2 + (c + d) % 2 for r in range(RING)]

    def arrange(weight, d):
        parts = [lax.dynamic_slice_in_dim(weight, s * features, features, 1) for s in sections(d)]
        return jnp.concatenate(parts, axis=1)

    w_down = [arrange(down_weight[0], d) for d in range(2)]
    w_both = [
        jnp.concatenate([arrange(gate_weight[0], d), arrange(up_weight[0], d)], axis=0)
        for d in range(2)
    ]

    def gather_y(rows):
        from_left, from_right = turn(rows, "y", 1), turn(rows, "y", -1)
        far_top = turn(from_left[: block // 2], "y", 1)
        far_bottom = turn(from_right[block // 2 :], "y", -1)
        own = [rows, from_right, jnp.concatenate([far_top, far_bottom], axis=0), from_left]
        return own, far_top, far_bottom

    dy_own, dy_top, dy_bottom = gather_y(dy_rows)
    dy_other = [swap(rows, "c") for rows in dy_own]
    x_rows = gather_z(after(x_rows, dy_own[0]))
    x_rows = after(x_rows, dy_own[1], dy_own[3])
    x_own, x_top, x_bottom = gather_y(x_rows)
    x_other = [swap(rows, "c") for rows in x_own]

    contract_last = (((1,), (1,)), ((), ()))
    contract_first = (((0,), (0,)), ((), ()))
    grads, scores, dx = [None] * RING, [None] * RING, [None] * RING
    for k in (0, 1, 3, 2):
        span = slice(k * block, (k + 1) * block)
        pull_back = lax.dot_general(w_down[0], dy_own[k], contract_last, preferred_element_type=F32)
        pull_back = pull_back + lax.dot_general(
            w_down[1], dy_other[k], contract_last, preferred_element_type=F32
        )
        scores[k] = jnp.sum(hidden[:, span].astype(F32) * pull_back, axis=0)
        d_gate = (pull_back * gate_slope[:, span]).astype(BF16)
        d_up = (pull_back * activated[:, span]).astype(BF16)
        grads[k] = jnp.concatenate([d_gate, d_up], axis=0)
    for k in (2, 1, 3, 0):
        own, other = (
            lax.dot_general(grads[k], w_both[d], contract_first, preferred_element_type=F32).astype(BF16)
            for d in range(2)
        )
        dx[k] = own.astype(F32) + swap(other, "c").astype(F32)

    far = dx[2].astype(BF16)
    from_left = turn(far[: block // 2], "y", 1).astype(F32)
    from_right = turn(far[block // 2 :], "y", -1).astype(F32)
    right = jnp.concatenate([dx[1][: block // 2] + from_left, dx[1][block // 2 :]], axis=0)
    left = jnp.concatenate([dx[3][: block // 2], dx[3][block // 2 :] + from_right], axis=0)
    own_dx = dx[0] + turn(right.astype(BF16), "y", 1).astype(F32)
    own_dx = (own_dx + turn(left.astype(BF16), "y", -1).astype(F32)).astype(BF16)
    part = own_dx[:, :features].astype(F32)
    for r in range(1, RING):
        part = part + turn(own_dx[:, r * features : (r + 1) * features], "z", -r).astype(F32)
    back_dx = exchange(part.astype(BF16), -1)

    own_score = scores[0]
    for k in range(1, RING):
        own_score = own_score + turn(scores[k], "y", k)
    own_score = sum_ring(sum_pair(own_score, "c"), "z")
    back_score = exchange_small(own_score, -1)
    first_grad = jnp.sum(jnp.where(first_pick, back_score[None, :], 0.0), axis=1)
    second_grad = jnp.sum(jnp.where(second_pick, back_score[None, :], 0.0), axis=1)
    logit_step = (first_grad - second_grad) * first_share * (1.0 - first_share)
    logit_grad = pair_hot * logit_step[:, None]
    router_term = lax.dot_general(
        logit_grad, normed_input.astype(F32), contract_first, precision=lax.Precision.HIGHEST
    )
    raw_router = sum_pair(sum_ring(sum_ring(router_term, "y"), "x"), "h")
    row_count = features // (8 * RING)
    raw_router = lax.dynamic_slice_in_dim(
        raw_router, ((x * 2 + h) * RING + y) * row_count, row_count, 1
    ).T

    token_dx = jnp.dot(gate_matrix, back_dx.astype(F32), precision=lax.Precision.HIGHEST)
    input_grad = (
        token_dx
        + lax.dot_general(
            logit_grad, router_rows.astype(F32), contract_last, precision=lax.Precision.HIGHEST
        )
    ).astype(BF16)

    gate_all = jnp.concatenate(gate_rows)
    gated_hidden = (hidden.astype(F32) * gate_all[None, :]).astype(BF16)
    grad_all = jnp.concatenate(grads, axis=1)
    square_sum = jnp.sum(raw_router * raw_router)
    raw_down, raw_both = [], []
    for d, (dy_k, x_k) in enumerate(((dy_own, x_own), (dy_other, x_other))):
        raw = jnp.dot(gated_hidden, jnp.concatenate(dy_k, axis=0), preferred_element_type=F32)
        square_sum = square_sum + jnp.sum(raw * raw)
        raw_down.append(raw.astype(BF16))
    for d, (dy_k, x_k) in enumerate(((dy_own, x_own), (dy_other, x_other))):
        raw = jnp.dot(grad_all, jnp.concatenate(x_k, axis=0), preferred_element_type=F32)
        square_sum = square_sum + jnp.sum(raw * raw)
        raw_both.append(raw.astype(BF16))
    square_sum = jnp.full((8, 128), square_sum)
    square_sum = sum_pair(sum_ring(sum_ring(square_sum, "y"), "x"), "h")
    square_sum = sum_ring(sum_pair(square_sum, "c"), "z")[0, 0]
    entry_count = 3.0 * experts * hidden_dev * 8 * RING * width + 1.0 * width * experts
    factor = 1.0 / jnp.maximum(jnp.sqrt(square_sum / entry_count), 1.0)

    def finish(own, other):
        whole = jnp.stack([own.reshape(-1, RING, features), other.reshape(-1, RING, features)])
        parts = []
        for s in range(8):
            d = (s % 2 + c) % 2
            r = (z - s // 2) % RING
            piece = lax.dynamic_slice(whole, (d, 0, r, 0), (1, own.shape[0], 1, features))
            parts.append(piece.reshape(own.shape[0], features))
        return (factor * jnp.concatenate(parts, axis=1).astype(F32)).astype(BF16)[None]

    grad_down = finish(raw_down[0], raw_down[1])
    grad_gate = finish(raw_both[0][:hidden_dev], raw_both[1][:hidden_dev])
    grad_up = finish(raw_both[0][hidden_dev:], raw_both[1][hidden_dev:])
    return (input_grad, factor * raw_router, grad_gate, grad_up, grad_down)


def solution(mesh):
    fine = Mesh(mesh.devices.reshape(4, 2, 4, 2, 4), ("z", "c", "x", "h", "y"))
    section, expert, edata = ("z", "c"), ("x", "h"), "y"
    rows = P((*expert, edata), section)
    ids = P((*expert, edata), None)
    weight = P(expert, (*section, edata), None)
    in_specs = (rows, rows, ids, ids, P(), weight, weight, weight, weight, weight)
    out_specs = (rows, P((*section, *expert, edata), None), weight, weight, weight)
    return jax.shard_map(local, mesh=fine, in_specs=in_specs, out_specs=out_specs, check_vma=False)
```

```python
import functools

import jax
import jax.numpy as jnp
from jax import lax
from jax.experimental import pallas as pl
from jax.experimental.pallas import tpu as pltpu
from jax.sharding import Mesh, PartitionSpec as P

F32 = jnp.float32
BF16 = jnp.bfloat16
RING = 4
PIECES = 8
LANES = 128
TURN_RIGHT = (((1,), (1,)), ((), ()))
TURN_LEFT = (((0,), (0,)), ((), ()))


def turn(value, axis, step):
    return lax.ppermute(value, axis, [(i, (i + step) % RING) for i in range(RING)])


def swap(value, axis):
    return lax.ppermute(value, axis, [(0, 1), (1, 0)])


def sum_ring(value, axis):
    for bit in (1, 2):
        value = value + lax.ppermute(value, axis, [(i, i ^ bit) for i in range(RING)])
    return value


def sum_pair(value, axis):
    return value + swap(value, axis)


def after(value, *others):
    return lax.optimization_barrier((value,) + others)[0]


def params():
    return pltpu.CompilerParams(vmem_limit_bytes=44 * 2**20)


def pull_kernel(count, *refs):
    rows, own, other, out = refs[:count], refs[count], refs[count + 1], refs[count + 2]
    start = 0
    for ref in rows:
        size = ref.shape[0]
        for d, weight in enumerate((own, other)):
            out[d, start : start + size, :] = lax.dot_general(
                ref[...], weight[...], TURN_RIGHT, preferred_element_type=F32
            )
        start += size


def pull_call(rows, own, other):
    hidden_dev, half = own.shape
    total = sum(r.shape[0] for r in rows)
    return pl.pallas_call(
        functools.partial(pull_kernel, len(rows)),
        out_shape=jax.ShapeDtypeStruct((2, total, hidden_dev), F32),
        compiler_params=params(),
        cost_estimate=pl.CostEstimate(
            flops=4 * total * half * hidden_dev,
            bytes_accessed=2 * total * half + 4 * half * hidden_dev + 8 * total * hidden_dev,
            transcendentals=0,
        ),
        name="pull",
    )(*rows, own, other)


def slots_kernel(*refs):
    pulls, (active, slope, hidden), weights = refs[:4], refs[4:7], refs[7:11]
    outs, (d_gate, d_up, score) = refs[11 : 11 + PIECES], refs[11 + PIECES :]
    near_rows = pulls[0].shape[1]
    piece, half = outs[0].shape
    for i, out in enumerate(outs):
        span = slice(i * piece, (i + 1) * piece)
        mine, theirs = pulls[:2] if i * piece < near_rows else pulls[2:]
        first = i * piece % near_rows
        own_span = slice(first, first + piece)
        total, terms = None, []
        for d in range(2):
            pull = mine[d, own_span, :] + theirs[1 - d, own_span, :]
            point = jnp.sum(hidden[d, span, :].astype(F32) * pull, axis=1, keepdims=True)
            total = point if total is None else total + point
            gate_part = (pull * slope[d, span, :]).astype(BF16)
            up_part = (pull * active[d, span, :]).astype(BF16)
            d_gate[d, span, :] = gate_part
            d_up[d, span, :] = up_part
            terms += [(gate_part, weights[d]), (up_part, weights[2 + d])]
        score[span, :] = total
        step = min(512, half)
        for n in range(0, half, step):
            value = None
            for left, weight in terms:
                term = jnp.dot(left, weight[:, n : n + step], preferred_element_type=F32)
                value = term if value is None else value + term
            out[:, n : n + step] = value.astype(BF16)


def slots_call(pulls, active, slope, hidden, weights):
    _, total, hidden_dev = active.shape
    half = weights[0].shape[1]
    piece = total // PIECES
    shape = jax.ShapeDtypeStruct
    out = pl.pallas_call(
        slots_kernel,
        out_shape=[shape((piece, half), BF16)] * PIECES
        + [shape((2, total, hidden_dev), BF16)] * 2
        + [shape((total, 1), F32)],
        compiler_params=params(),
        cost_estimate=pl.CostEstimate(
            flops=8 * total * half * hidden_dev,
            bytes_accessed=2 * total * half + 8 * half * hidden_dev + 44 * total * hidden_dev,
            transcendentals=0,
        ),
        name="slots",
    )(*pulls, active, slope, hidden, *weights)
    return out[:PIECES], out[PIECES], out[PIECES + 1], out[PIECES + 2]


def grads_kernel(row_count, left_count, gate_count, *refs):
    rows, refs = refs[:row_count], refs[row_count:]
    gates, refs = refs[:gate_count], refs[gate_count:]
    lefts, refs = refs[:left_count], refs[left_count:]
    outs, square = refs[: 2 * left_count], refs[2 * left_count]
    right = jnp.concatenate([r[...] for r in rows], axis=0)
    total = jnp.zeros((8, right.shape[1]), F32)
    if gates:
        gate = jnp.concatenate([g[:, 0:1] for g in gates], axis=0).astype(F32)
    for i, left in enumerate(lefts):
        for d in range(2):
            value = left[d]
            if gates:
                value = (value.astype(F32) * gate).astype(BF16)
            raw = lax.dot_general(value, right, TURN_LEFT, preferred_element_type=F32)
            outs[2 * i + d][...] = raw.astype(BF16)
            total = total + jnp.sum((raw * raw).reshape(-1, 8, raw.shape[1]), axis=0)

    @pl.when(pl.program_id(0) == 0)
    def _():
        square[...] = jnp.zeros_like(square)

    square[...] += total


def grads_call(rows, gates, lefts, half):
    _, total, hidden_dev = lefts[0].shape
    step = min(512, half)
    shape = jax.ShapeDtypeStruct
    in_specs = [pl.BlockSpec((r.shape[0], step), lambda j: (0, j)) for r in rows]
    in_specs += [pl.BlockSpec((g.shape[0], LANES), lambda j: (0, half // LANES)) for g in gates]
    in_specs += [pl.BlockSpec((2, total, hidden_dev), lambda j: (0, 0, 0))] * len(lefts)
    out = pl.pallas_call(
        functools.partial(grads_kernel, len(rows), len(lefts), len(gates)),
        grid=(half // step,),
        in_specs=in_specs,
        out_specs=[pl.BlockSpec((hidden_dev, step), lambda j: (0, j))] * (2 * len(lefts))
        + [pl.BlockSpec((8, step), lambda j: (0, 0))],
        out_shape=[shape((hidden_dev, half), BF16)] * (2 * len(lefts)) + [shape((8, step), F32)],
        compiler_params=params(),
        cost_estimate=pl.CostEstimate(
            flops=4 * len(lefts) * total * half * hidden_dev,
            bytes_accessed=2 * total * half + 4 * len(lefts) * (half + total) * hidden_dev,
            transcendentals=0,
        ),
        name="grads",
    )(*rows, *gates, *lefts)
    return out[0:-1:2], out[1:-1:2], jnp.sum(out[-1])


def local(
    normed_input,
    output_grad,
    expert_ids,
    slot_pos,
    router_weight,
    gate_weight,
    up_weight,
    down_weight,
    saved_gate,
    saved_up,
):
    z, c, x, h, y = (lax.axis_index(name) for name in ("z", "c", "x", "h", "y"))
    width, experts = router_weight.shape
    tokens, features = normed_input.shape
    hidden_dev = gate_weight.shape[1]
    slot_total = saved_gate.shape[2]
    capacity = slot_total // (8 * RING)
    piece = RING * capacity
    block = 2 * piece
    half = RING * features

    near_expert = ((expert_ids % 2 + h) % 2) * RING + (expert_ids // 2 - x) % RING
    live_mask = slot_pos < capacity
    address = near_expert * capacity + slot_pos
    table = jnp.arange(block, dtype=jnp.int32)[None, :]
    first_pick = (address[:, 0:1] == table) & live_mask[:, 0:1]
    second_pick = (address[:, 1:2] == table) & live_mask[:, 1:2]
    pick_matrix = (first_pick | second_pick).astype(BF16)

    def place(matrix, values):
        return lax.dot_general(matrix, values, TURN_LEFT, preferred_element_type=F32).astype(BF16)

    def exchange_x(rows, sign):
        parts = rows.reshape(2, RING, capacity, -1)
        out = [parts[:, 0]] + [turn(parts[:, a], "x", sign * a) for a in range(1, RING)]
        return [jnp.concatenate([part[b] for part in out], axis=0) for b in range(2)]

    def gather_z(rows):
        return jnp.concatenate([rows] + [turn(rows, "z", r) for r in range(1, RING)], axis=1)

    near, far = exchange_x(place(pick_matrix, output_grad), 1)
    far = swap(far, "h")
    near = gather_z(near)
    far = gather_z(far)
    near_left, near_right = turn(near, "y", 1), turn(near, "y", -1)
    far_left, far_right = turn(far, "y", 1), turn(far, "y", -1)
    across = turn(near_left, "y", 1), turn(far_right, "y", -1)
    dy_pieces = [near, far, near_right, far_right, near_left, far_left]

    router_rows = lax.dynamic_slice_in_dim(router_weight, (z * 2 + c) * features, features, 0)
    logits = jnp.dot(normed_input, router_rows, preferred_element_type=F32)
    logits = sum_ring(sum_pair(logits, "c"), "z")
    columns = jnp.arange(experts, dtype=jnp.int32)[None, :]
    first_hot = (columns == expert_ids[:, 0:1]).astype(F32)
    second_hot = (columns == expert_ids[:, 1:2]).astype(F32)
    pair_hot = first_hot - second_hot
    first_share = jax.nn.sigmoid(
        jnp.sum(logits * first_hot, axis=1) - jnp.sum(logits * second_hot, axis=1)
    )
    gate_first = first_share.astype(BF16).astype(F32)
    gate_second = (1.0 - first_share).astype(BF16).astype(F32)
    gate_matrix = jnp.where(first_pick, gate_first[:, None], 0.0) + jnp.where(
        second_pick, gate_second[:, None], 0.0
    )

    def arrange(weight, d):
        parts = [
            lax.dynamic_slice_in_dim(
                weight, (((z - r) % RING) * 2 + (c + d) % 2) * features, features, 1
            )
            for r in range(RING)
        ]
        return jnp.concatenate(parts, axis=1)

    three = [down_weight[0], gate_weight[0], up_weight[0]]
    own_weights = [arrange(w, 0) for w in three]
    other_weights = swap(jnp.stack([arrange(w, 1) for w in three]), "c")
    saved = jnp.concatenate([saved_gate, saved_up], axis=0)
    saved = jnp.concatenate([saved, swap(saved, "c")], axis=0).reshape(-1, slot_total)
    order = jnp.arange(slot_total, dtype=jnp.int32)
    turn_y = order // block
    from_y = (y + jnp.where(turn_y < 2, turn_y, 5 - turn_y)) % RING
    from_h = (h + (order // piece) % 2) % 2
    from_x = (x - (order // capacity) % RING) % RING
    source = ((from_x * 2 + from_h) * RING + from_y) * capacity + order % capacity
    shuffle = (source[:, None] == order[None, :]).astype(BF16)
    saved = lax.dot_general(
        saved.reshape(4, hidden_dev, slot_total), shuffle, (((2,), (1,)), ((), ())), preferred_element_type=F32
    ).transpose(0, 2, 1)
    pre_gate, pre_up = saved[0::2], saved[1::2]
    sigmoid_gate = jax.nn.sigmoid(pre_gate)
    active = pre_gate * sigmoid_gate
    hidden = (active * pre_up).astype(BF16)
    slope = pre_up * (sigmoid_gate * (1.0 + pre_gate * (1.0 - sigmoid_gate)))

    gated = jnp.concatenate([normed_input, jnp.ones((tokens, LANES), BF16)], axis=1)
    x_near, x_far = exchange_x(place(gate_matrix.astype(BF16), gated), 1)
    x_near, x_far = after((x_near, x_far), near, far)
    x_rows = jnp.concatenate([x_near, swap(x_far, "h")], axis=0)
    x_rows = jnp.concatenate([gather_z(x_rows[:, :features]), x_rows[:, features:]], axis=1)
    x_rows = after(x_rows, *across)
    x_left, x_right = turn(x_rows, "y", 1), turn(x_rows, "y", -1)
    x_across = turn(x_left[:piece], "y", 1), turn(x_right[piece:], "y", -1)
    x_pieces = [x_rows, x_right, x_left, *x_across]

    pulls = []
    for rows in (dy_pieces, list(across)):
        pull = pull_call(rows, own_weights[0], other_weights[0])
        pulls += [pull, swap(pull, "c")]
    weights = [own_weights[1], other_weights[1], own_weights[2], other_weights[2]]
    dx, d_gate, d_up, score = slots_call(pulls, active, slope, hidden, weights)

    score = score.reshape(RING, block)
    score = jnp.stack([score[0], score[1], score[3], score[2]])
    score = score[:2] + turn(score[2:], "y", 2)
    score = sum_ring(score[0] + turn(score[1], "y", 1), "z").reshape(2, RING, capacity)
    score = jnp.stack([score[0], swap(score[1], "h")])
    score = jnp.concatenate([score[:, :2], turn(score[:, 2:], "x", -2)], axis=1)
    odd = turn(score[:, 1::2], "x", -1)
    score = jnp.stack([score[:, 0], odd[:, 0], score[:, 2], odd[:, 1]], axis=1).reshape(1, block)
    first_grad = jnp.sum(jnp.where(first_pick, score, 0.0), axis=1)
    second_grad = jnp.sum(jnp.where(second_pick, score, 0.0), axis=1)
    logit_step = (first_grad - second_grad) * first_share * (1.0 - first_share)
    logit_grad = pair_hot * logit_step[:, None]
    router_term = lax.dot_general(
        logit_grad, normed_input.astype(F32), TURN_LEFT, precision=lax.Precision.HIGHEST
    )

    def add(*terms):
        return functools.reduce(lambda a, b: a + b, [t.astype(F32) for t in terms])

    dx = after(dx, *x_across)
    to_right = add(dx[2], turn(dx[6], "y", 1)).astype(BF16)
    to_left = add(dx[5], turn(dx[7], "y", -1)).astype(BF16)
    back = []
    for own, right, left in ((dx[1], dx[3], to_left), (dx[0], to_right, dx[4])):
        own = add(own, turn(right, "y", 1), turn(left, "y", -1)).astype(BF16)
        parts = [turn(own[:, r * features : (r + 1) * features], "z", -r) for r in range(1, RING)]
        back.append(add(own[:, :features], *parts).astype(BF16))
    far, near = back
    far = swap(far, "h")
    back_dx = jnp.concatenate(exchange_x(jnp.concatenate([near, far], axis=0), -1), axis=0)
    token_dx = jnp.dot(gate_matrix, back_dx.astype(F32), precision=lax.Precision.HIGHEST)
    input_grad = (
        token_dx
        + lax.dot_general(
            logit_grad, router_rows.astype(F32), TURN_RIGHT, precision=lax.Precision.HIGHEST
        )
    ).astype(BF16)

    (own_down,), (other_down,), down_square = grads_call(
        dy_pieces + list(across), x_pieces, [hidden], half
    )
    own_two, other_two, two_square = grads_call(x_pieces, [], [d_gate, d_up], half)
    other_down = swap(other_down, "c")
    other_two = swap(jnp.stack(other_two), "c")

    message = jnp.concatenate(
        [router_term, jnp.full((8, features), down_square + two_square, F32)], axis=0
    )
    message = sum_pair(sum_ring(sum_ring(message, "y"), "x"), "h")
    raw_router = message[:experts]
    square_sum = jnp.full((8, LANES), message[experts, 0] + jnp.sum(raw_router * raw_router), F32)
    square_sum = sum_ring(sum_pair(square_sum, "c"), "z")[0, 0]
    row_count = features // (8 * RING)
    raw_router = lax.dynamic_slice_in_dim(
        raw_router, ((x * 2 + h) * RING + y) * row_count, row_count, 1
    ).T
    entry_count = 3.0 * experts * hidden_dev * 8 * RING * width + 1.0 * width * experts
    factor = 1.0 / jnp.maximum(jnp.sqrt(square_sum / entry_count), 1.0)

    def finish(own, other):
        whole = jnp.stack([own.reshape(-1, RING, features), other.reshape(-1, RING, features)])
        parts = []
        for s in range(8):
            d = (s % 2 + c) % 2
            r = (z - s // 2) % RING
            part = lax.dynamic_slice(whole, (d, 0, r, 0), (1, own.shape[0], 1, features))
            parts.append(part.reshape(own.shape[0], features))
        return (factor * jnp.concatenate(parts, axis=1).astype(F32)).astype(BF16)[None]

    grad_down = finish(own_down, other_down)
    grad_gate = finish(own_two[0], other_two[0])
    grad_up = finish(own_two[1], other_two[1])
    return (input_grad, factor * raw_router, grad_gate, grad_up, grad_down)


def solution(mesh):
    fine = Mesh(mesh.devices.reshape(4, 2, 4, 2, 4), ("z", "c", "x", "h", "y"))
    section, expert, edata = ("z", "c"), ("x", "h"), "y"
    rows = P((*expert, edata), section)
    ids = P((*expert, edata), None)
    weight = P(expert, (*section, edata), None)
    in_specs = (rows, rows, ids, ids, P(), weight, weight, weight, weight, weight)
    out_specs = (rows, P((*section, *expert, edata), None), weight, weight, weight)
    return jax.shard_map(local, mesh=fine, in_specs=in_specs, out_specs=out_specs, check_vma=False)
```

```python
import functools

import jax
import jax.numpy as jnp
from jax import lax
from jax.experimental import pallas as pl
from jax.experimental.pallas import tpu as pltpu
from jax.sharding import Mesh, PartitionSpec as P

F32 = jnp.float32
BF16 = jnp.bfloat16
RING = 4
PIECES = 8
LANES = 128
TURN_RIGHT = (((1,), (1,)), ((), ()))
TURN_LEFT = (((0,), (0,)), ((), ()))


def turn(value, axis, step):
    return lax.ppermute(value, axis, [(i, (i + step) % RING) for i in range(RING)])


def swap(value, axis):
    return lax.ppermute(value, axis, [(0, 1), (1, 0)])


def sum_ring(value, axis):
    for bit in (1, 2):
        value = value + lax.ppermute(value, axis, [(i, i ^ bit) for i in range(RING)])
    return value


def sum_pair(value, axis):
    return value + swap(value, axis)


def after(value, *others):
    return lax.optimization_barrier((value,) + others)[0]


def params():
    return pltpu.CompilerParams(vmem_limit_bytes=60 * 2**20)


def cost():
    return pl.CostEstimate(flops=1, bytes_accessed=1, transcendentals=0)


def whole_lanes(count):
    return -(-count // LANES) * LANES


def pull_kernel(count, *refs):
    rows, weights, out = refs[:count], refs[count : count + 2], refs[count + 2]
    hidden_dev = weights[0].shape[0]

    @pl.when(pl.program_id(0) == 0)
    def _():
        out[...] = jnp.zeros_like(out)

    start = 0
    for ref in rows:
        size = ref.shape[0]
        for d, weight in enumerate(weights):
            out[d, start : start + size, :hidden_dev] += lax.dot_general(
                ref[...], weight[...], TURN_RIGHT, preferred_element_type=F32
            )
        start += size


def pull_call(rows, own, other):
    _, hidden_dev, half = own.shape
    total = sum(r.shape[0] for r in rows)
    step = min(512, half)
    lanes = whole_lanes(hidden_dev)
    weight = pl.BlockSpec((None, hidden_dev, step), lambda i: (0, 0, i))
    return pl.pallas_call(
        functools.partial(pull_kernel, len(rows)),
        grid=(half // step,),
        in_specs=[pl.BlockSpec((r.shape[0], step), lambda i: (0, i)) for r in rows] + [weight] * 2,
        out_specs=pl.BlockSpec((2, total, lanes), lambda i: (0, 0, 0)),
        out_shape=jax.ShapeDtypeStruct((2, total, lanes), F32),
        compiler_params=params(),
        cost_estimate=cost(),
        name="pull",
    )(*rows, own, other)


def slots_kernel(near, *refs):
    pulls, (active, slope, hidden), weights = refs[:4], refs[4:7], refs[7:11]
    outs, (d_gate, d_up, score, value_ref) = refs[11 : 11 + PIECES], refs[11 + PIECES :]
    step = pl.program_id(0)
    half = outs[0].shape[1]
    hidden_dev = active.shape[2]
    total, terms = None, []
    for d in range(2):
        near_pull = pulls[0][d] + pulls[1][1 - d]
        far_pull = pulls[2][d] + pulls[3][1 - d]
        pull = jnp.where(step < near, near_pull, far_pull)[:, :hidden_dev]
        point = jnp.sum(hidden[d].astype(F32) * pull, axis=1, keepdims=True)
        total = point if total is None else total + point
        gate_part = (pull * slope[d]).astype(BF16)
        up_part = (pull * active[d]).astype(BF16)
        d_gate[d] = gate_part
        d_up[d] = up_part
        terms += [(gate_part, weights[2 * d]), (up_part, weights[2 * d + 1])]
    score[...] = total
    run = min(512, half)
    for n in range(0, half, run):
        value = None
        for left, weight in terms:
            term = jnp.dot(left, weight[:, n : n + run], preferred_element_type=F32)
            value = term if value is None else value + term
        value_ref[:, n : n + run] = value.astype(BF16)

    def write(i):
        outs[i][...] = value_ref[...]

    for i in range(PIECES):
        pl.when(step == i)(functools.partial(write, i))


def slots_call(pulls, active, slope, hidden, own, other):
    _, total, hidden_dev = active.shape
    half = own.shape[2]
    piece = total // PIECES
    near, lanes = pulls[0].shape[1] // piece, pulls[0].shape[2]
    shape = jax.ShapeDtypeStruct
    near_spec = pl.BlockSpec((2, piece, lanes), lambda i: (0, jnp.minimum(i, near - 1), 0))
    far_spec = pl.BlockSpec((2, piece, lanes), lambda i: (0, jnp.maximum(i - near, 0), 0))
    units = pl.BlockSpec((2, piece, hidden_dev), lambda i: (0, i, 0))
    gate = pl.BlockSpec((None, hidden_dev, half), lambda i: (1, 0, 0))
    up = pl.BlockSpec((None, hidden_dev, half), lambda i: (2, 0, 0))
    out = pl.pallas_call(
        functools.partial(slots_kernel, near),
        grid=(PIECES,),
        in_specs=[near_spec, near_spec, far_spec, far_spec, units, units, units, gate, up, gate, up],
        out_specs=[pl.BlockSpec((piece, half), lambda i: (0, 0))] * PIECES
        + [units, units, pl.BlockSpec((piece, 1), lambda i: (i, 0))],
        out_shape=[shape((piece, half), BF16)] * PIECES
        + [shape((2, total, hidden_dev), BF16)] * 2
        + [shape((total, 1), F32)],
        scratch_shapes=[pltpu.VMEM((piece, half), BF16)],
        compiler_params=params(),
        cost_estimate=cost(),
        name="slots",
    )(*pulls, active, slope, hidden, own, own, other, other)
    return out[:PIECES], out[PIECES], out[PIECES + 1], out[PIECES + 2]


def arrange_kernel(place, *refs):
    weights, outs = refs[:3], refs[3:]
    features = outs[0].shape[2]

    def copy(core):
        for d, out in enumerate(outs):
            first = (core + d) % 2 * features
            for i, weight in enumerate(weights):
                out[i] = weight[:, first : first + features]

    for core in range(2):
        pl.when(place[RING] == core)(functools.partial(copy, core))


def arrange_call(place, weights, features):
    hidden_dev, width = weights[0].shape
    shape = jax.ShapeDtypeStruct((3, hidden_dev, RING * features), BF16)
    block = (3, hidden_dev, features)
    return pl.pallas_call(
        arrange_kernel,
        grid_spec=pltpu.PrefetchScalarGridSpec(
            num_scalar_prefetch=1,
            grid=(RING,),
            in_specs=[pl.BlockSpec((hidden_dev, 2 * features), lambda r, t: (0, t[r]))] * 3,
            out_specs=[pl.BlockSpec(block, lambda r, t: (0, 0, r))] * 2,
        ),
        out_shape=[shape, shape],
        compiler_params=params(),
        cost_estimate=cost(),
        name="arrange",
    )(place, *weights)


def finish_kernel(place, factor, *refs):
    ins, outs = refs[:6], refs[6:]
    features = ins[0].shape[1]

    def write(core):
        for d in range(2):
            first = (core + d) % 2 * features
            for i, out in enumerate(outs):
                value = factor[0] * ins[2 * i + d][...].astype(F32)
                out[:, first : first + features] = value.astype(BF16)

    for core in range(2):
        pl.when(place[RING] == core)(functools.partial(write, core))


def finish_call(place, factor, pairs, features):
    hidden_dev, half = pairs[0][0].shape
    return pl.pallas_call(
        finish_kernel,
        grid_spec=pltpu.PrefetchScalarGridSpec(
            num_scalar_prefetch=1,
            grid=(RING,),
            in_specs=[pl.BlockSpec(memory_space=pltpu.SMEM)]
            + [pl.BlockSpec((hidden_dev, features), lambda r, t: (0, r))] * 6,
            out_specs=[pl.BlockSpec((None, hidden_dev, 2 * features), lambda r, t: (0, 0, t[r]))] * 3,
        ),
        out_shape=[jax.ShapeDtypeStruct((1, hidden_dev, 2 * half), BF16)] * 3,
        compiler_params=params(),
        cost_estimate=cost(),
        name="finish",
    )(place, factor, *[p for pair in pairs for p in pair])


def grads_kernel(row_count, left_count, gate_count, *refs):
    rows, refs = refs[:row_count], refs[row_count:]
    gates, refs = refs[:gate_count], refs[gate_count:]
    lefts, refs = refs[:left_count], refs[left_count:]
    outs, square = refs[: 2 * left_count], refs[2 * left_count]
    right = jnp.concatenate([r[...] for r in rows], axis=0)
    total = jnp.zeros((8, right.shape[1]), F32)
    if gates:
        gate = jnp.concatenate([g[:, 0:1] for g in gates], axis=0).astype(F32)
    for i, left in enumerate(lefts):
        for d in range(2):
            value = left[d]
            if gates:
                value = (value.astype(F32) * gate).astype(BF16)
            raw = lax.dot_general(value, right, TURN_LEFT, preferred_element_type=F32)
            outs[2 * i + d][...] = raw.astype(BF16)
            total = total + jnp.sum((raw * raw).reshape(-1, 8, raw.shape[1]), axis=0)

    @pl.when(pl.program_id(0) == 0)
    def _():
        square[...] = jnp.zeros_like(square)

    square[...] += total


def grads_call(rows, gates, lefts, half):
    _, total, hidden_dev = lefts[0].shape
    step = min(512, half)
    shape = jax.ShapeDtypeStruct
    in_specs = [pl.BlockSpec((r.shape[0], step), lambda j: (0, j)) for r in rows]
    in_specs += [pl.BlockSpec((g.shape[0], LANES), lambda j: (0, half // LANES)) for g in gates]
    in_specs += [pl.BlockSpec((2, total, hidden_dev), lambda j: (0, 0, 0))] * len(lefts)
    out = pl.pallas_call(
        functools.partial(grads_kernel, len(rows), len(lefts), len(gates)),
        grid=(half // step,),
        in_specs=in_specs,
        out_specs=[pl.BlockSpec((hidden_dev, step), lambda j: (0, j))] * (2 * len(lefts))
        + [pl.BlockSpec((8, step), lambda j: (0, 0))],
        out_shape=[shape((hidden_dev, half), BF16)] * (2 * len(lefts)) + [shape((8, step), F32)],
        compiler_params=params(),
        cost_estimate=cost(),
        name="grads",
    )(*rows, *gates, *lefts)
    return out[0:-1:2], out[1:-1:2], jnp.sum(out[-1])


def local(
    normed_input,
    output_grad,
    expert_ids,
    slot_pos,
    router_weight,
    gate_weight,
    up_weight,
    down_weight,
    saved_gate,
    saved_up,
):
    z, c, x, h, y = (lax.axis_index(name) for name in ("z", "c", "x", "h", "y"))
    width, experts = router_weight.shape
    tokens, features = normed_input.shape
    hidden_dev = gate_weight.shape[1]
    slot_total = saved_gate.shape[2]
    capacity = slot_total // (8 * RING)
    piece = RING * capacity
    block = 2 * piece
    half = RING * features

    near_expert = ((expert_ids % 2 + h) % 2) * RING + (expert_ids // 2 - x) % RING
    live_mask = slot_pos < capacity
    address = near_expert * capacity + slot_pos
    table = jnp.arange(block, dtype=jnp.int32)[None, :]
    first_pick = (address[:, 0:1] == table) & live_mask[:, 0:1]
    second_pick = (address[:, 1:2] == table) & live_mask[:, 1:2]
    pick_matrix = (first_pick | second_pick).astype(BF16)

    def place(matrix, values):
        return lax.dot_general(matrix, values, TURN_LEFT, preferred_element_type=F32).astype(BF16)

    def exchange_x(rows, sign):
        parts = rows.reshape(2, RING, capacity, -1)
        out = [parts[:, 0]] + [turn(parts[:, a], "x", sign * a) for a in range(1, RING)]
        return [jnp.concatenate([part[b] for part in out], axis=0) for b in range(2)]

    def gather_z(rows):
        return jnp.concatenate([rows] + [turn(rows, "z", r) for r in range(1, RING)], axis=1)

    def add(*terms):
        return functools.reduce(lambda a, b: a + b, [t.astype(F32) for t in terms])

    barrier = lax.optimization_barrier

    dy_placed = place(pick_matrix, output_grad)
    near, far = exchange_x(dy_placed, 1)
    router_rows = lax.dynamic_slice_in_dim(router_weight, (z * 2 + c) * features, features, 0)
    logits = jnp.dot(normed_input, router_rows, preferred_element_type=F32)
    logits = sum_pair(after(logits, dy_placed), "c")
    near, far, logits = barrier((near, far, logits))

    far = swap(far, "h")
    near = gather_z(near)
    logits = sum_ring(logits, "z")
    columns = jnp.arange(experts, dtype=jnp.int32)[None, :]
    first_hot = (columns == expert_ids[:, 0:1]).astype(F32)
    second_hot = (columns == expert_ids[:, 1:2]).astype(F32)
    pair_hot = first_hot - second_hot
    first_share = jax.nn.sigmoid(
        jnp.sum(logits * first_hot, axis=1) - jnp.sum(logits * second_hot, axis=1)
    )
    gate_first = first_share.astype(BF16).astype(F32)
    gate_second = (1.0 - first_share).astype(BF16).astype(F32)
    gate_matrix = jnp.where(first_pick, gate_first[:, None], 0.0) + jnp.where(
        second_pick, gate_second[:, None], 0.0
    )
    gated = jnp.concatenate([normed_input, jnp.ones((tokens, LANES), BF16)], axis=1)
    x_placed = place(gate_matrix.astype(BF16), gated)
    far, x_placed = barrier((far, x_placed))

    far = gather_z(far)
    near_left, near_right = turn(near, "y", 1), turn(near, "y", -1)
    x_near, x_far = exchange_x(x_placed, 1)
    far, x_near, x_far = barrier((far, x_near, x_far))

    far_left, far_right = turn(far, "y", 1), turn(far, "y", -1)
    x_far = swap(x_far, "h")
    sections = jnp.stack([(z - r) % RING for r in range(RING)] + [c]).astype(jnp.int32)
    weights = after((down_weight[0], gate_weight[0], up_weight[0]), x_near)
    own_weights, other_weights = arrange_call(sections, weights, features)
    saved = after(jnp.concatenate([saved_gate, saved_up], axis=0), x_near)
    near_left, near_right, x_far, other_weights, saved = barrier(
        (near_left, near_right, x_far, other_weights, saved)
    )

    near_across = turn(near_left, "y", 1)
    x_rows = jnp.concatenate([x_near, x_far], axis=0)
    x_gates = x_rows[:, features:]
    x_rows = gather_z(x_rows[:, :features])
    other_weights = swap(other_weights, "c")
    saved = jnp.concatenate([saved, swap(saved, "c")], axis=0)
    far_across = turn(far_right, "y", -1)
    order = jnp.arange(slot_total, dtype=jnp.int32)
    turn_y = order // block
    from_y = (y + jnp.where(turn_y < 2, turn_y, 5 - turn_y)) % RING
    from_h = (h + (order // piece) % 2) % 2
    from_x = (x - (order // capacity) % RING) % RING
    source = ((from_x * 2 + from_h) * RING + from_y) * capacity + order % capacity
    shuffle = (source[:, None] == order[None, :]).astype(BF16)
    saved = lax.dot_general(
        saved, shuffle, (((2,), (1,)), ((), ())), preferred_element_type=F32
    ).transpose(0, 2, 1)
    pre_gate, pre_up = saved[0::2], saved[1::2]
    sigmoid_gate = jax.nn.sigmoid(pre_gate)
    active = pre_gate * sigmoid_gate
    hidden = (active * pre_up).astype(BF16)
    slope = pre_up * (sigmoid_gate * (1.0 + pre_gate * (1.0 - sigmoid_gate)))
    far_left, far_right, active, slope, hidden = barrier((far_left, far_right, active, slope, hidden))
    dy_pieces = [near, far, near_right, far_right, near_left, far_left]
    near_pull = pull_call(dy_pieces, own_weights, other_weights)
    near_across, far_across, x_rows = barrier((near_across, far_across, x_rows))
    across = [near_across, far_across]
    x_rows = jnp.concatenate([x_rows, x_gates], axis=1)

    x_left, x_right = turn(x_rows, "y", 1), turn(x_rows, "y", -1)
    far_pull = pull_call(across, own_weights, other_weights)
    pulls = [near_pull, swap(near_pull, "c"), far_pull, swap(far_pull, "c")]
    dx, d_gate, d_up, score = slots_call(pulls, active, slope, hidden, own_weights, other_weights)
    x_left, x_right, dx, score = barrier((x_left, x_right, dx, score))

    from_left, from_right = turn(dx[6], "y", 1), turn(dx[7], "y", -1)
    x_across = turn(x_left[:piece], "y", 1), turn(x_right[piece:], "y", -1)
    score = score.reshape(RING, block)
    score = jnp.stack([score[0], score[1], score[3], score[2]])
    score = score[:2] + turn(score[2:], "y", 2)
    score = score[0] + turn(score[1], "y", 1)
    score = sum_ring(score, "z").reshape(2, RING, capacity)
    from_left, from_right, x_across, score = barrier((from_left, from_right, x_across, score))
    x_pieces = [x_rows, x_right, x_left, *x_across]

    to_right = add(dx[2], from_left).astype(BF16)
    to_left = add(dx[5], from_right).astype(BF16)
    moved = [
        (turn(right, "y", 1), turn(left, "y", -1))
        for right, left in ((dx[3], to_left), (to_right, dx[4]))
    ]
    score = jnp.stack([score[0], swap(score[1], "h")])
    score = jnp.concatenate([score[:, :2], turn(score[:, 2:], "x", -2)], axis=1)
    odd = turn(score[:, 1::2], "x", -1)
    score = jnp.stack([score[:, 0], odd[:, 0], score[:, 2], odd[:, 1]], axis=1).reshape(1, block)
    hidden, d_gate, d_up = after((hidden, d_gate, d_up), to_right, to_left)
    (own_down,), (other_down,), down_square = grads_call(dy_pieces + across, x_pieces, [hidden], half)
    moved, score, down_square = barrier((moved, score, down_square))

    sums = [add(dx[1 - i], *pair).astype(BF16) for i, pair in enumerate(moved)]
    parts = [
        [turn(own[:, r * features : (r + 1) * features], "z", -r) for r in range(1, RING)] for own in sums
    ]
    first_grad = jnp.sum(jnp.where(first_pick, score, 0.0), axis=1)
    second_grad = jnp.sum(jnp.where(second_pick, score, 0.0), axis=1)
    logit_step = (first_grad - second_grad) * first_share * (1.0 - first_share)
    logit_grad = pair_hot * logit_step[:, None]
    router_term = lax.dot_general(
        logit_grad, normed_input.astype(F32), TURN_LEFT, precision=lax.Precision.HIGHEST
    )
    own_two, other_two, two_square = grads_call(x_pieces, [], after([d_gate, d_up], sums), half)
    message = jnp.concatenate(
        [router_term, jnp.full((8, features), down_square + two_square, F32)], axis=0
    )
    message = sum_ring(sum_ring(message, "y"), "x")
    other_down = swap(other_down, "c")
    other_two = [swap(part, "c") for part in other_two]
    parts, message = barrier((parts, message))
    far, near = [add(own[:, :features], *part).astype(BF16) for own, part in zip(sums, parts)]

    far = swap(far, "h")
    message = sum_pair(message, "h")
    raw_router = message[:experts]
    square_sum = jnp.full((8, LANES), message[experts, 0] + jnp.sum(raw_router * raw_router), F32)
    square_sum = sum_pair(square_sum, "c")
    far, square_sum = barrier((far, square_sum))
    back_dx = exchange_x(jnp.concatenate([near, far], axis=0), -1)
    square_sum = sum_ring(square_sum, "z")[0, 0]
    row_count = features // (8 * RING)
    raw_router = lax.dynamic_slice_in_dim(
        raw_router, ((x * 2 + h) * RING + y) * row_count, row_count, 1
    ).T
    back_dx = jnp.concatenate(back_dx, axis=0)
    token_dx = jnp.dot(gate_matrix, back_dx.astype(F32), precision=lax.Precision.HIGHEST)
    input_grad = (
        token_dx
        + lax.dot_general(
            logit_grad, router_rows.astype(F32), TURN_RIGHT, precision=lax.Precision.HIGHEST
        )
    ).astype(BF16)
    entry_count = 3.0 * experts * hidden_dev * 8 * RING * width + 1.0 * width * experts
    factor = 1.0 / jnp.maximum(jnp.sqrt(square_sum / entry_count), 1.0)
    pairs = [(own_two[0], other_two[0]), (own_two[1], other_two[1]), (own_down, other_down)]
    grad_gate, grad_up, grad_down = finish_call(sections, factor.reshape(1), pairs, features)
    return (input_grad, factor * raw_router, grad_gate, grad_up, grad_down)


def solution(mesh):
    fine = Mesh(mesh.devices.reshape(4, 2, 4, 2, 4), ("z", "c", "x", "h", "y"))
    section, expert, edata = ("z", "c"), ("x", "h"), "y"
    rows = P((*expert, edata), section)
    ids = P((*expert, edata), None)
    weight = P(expert, (*section, edata), None)
    in_specs = (rows, rows, ids, ids, P(), weight, weight, weight, weight, weight)
    out_specs = (rows, P((*section, *expert, edata), None), weight, weight, weight)
    return jax.shard_map(local, mesh=fine, in_specs=in_specs, out_specs=out_specs, check_vma=False)
```

```python
import functools

import jax
import jax.numpy as jnp
from jax import lax
from jax.experimental import pallas as pl
from jax.experimental.pallas import tpu as pltpu
from jax.sharding import Mesh, PartitionSpec as P

F32 = jnp.float32
BF16 = jnp.bfloat16
RING = 4
PIECES = 8
LANES = 128
TURN_RIGHT = (((1,), (1,)), ((), ()))
TURN_LEFT = (((0,), (0,)), ((), ()))


def turn(value, axis, step):
    return lax.ppermute(value, axis, [(i, (i + step) % RING) for i in range(RING)])


def swap(value, axis):
    return lax.ppermute(value, axis, [(0, 1), (1, 0)])


def sum_ring(value, axis):
    for bit in (1, 2):
        value = value + lax.ppermute(value, axis, [(i, i ^ bit) for i in range(RING)])
    return value


def sum_turns(value, axis):
    one, two, three = turn(value, axis, 1), turn(value, axis, 2), turn(value, axis, 3)
    return (value + two) + (one + three)


def sum_pair(value, axis):
    return value + swap(value, axis)


def after(value, *others):
    return lax.optimization_barrier((value,) + others)[0]


def params():
    return pltpu.CompilerParams(vmem_limit_bytes=60 * 2**20)


def cost():
    return pl.CostEstimate(flops=1, bytes_accessed=1, transcendentals=0)


def whole_lanes(count):
    return -(-count // LANES) * LANES


def pull_kernel(count, *refs):
    rows, weights, out = refs[:count], refs[count : count + 2], refs[count + 2]
    hidden_dev = weights[0].shape[0]

    @pl.when(pl.program_id(0) == 0)
    def _():
        out[...] = jnp.zeros_like(out)

    left = jnp.concatenate([ref[...] for ref in rows], axis=0)
    for d, weight in enumerate(weights):
        out[d, :, :hidden_dev] += lax.dot_general(left, weight[...], TURN_RIGHT, preferred_element_type=F32)


def pull_call(rows, own, other):
    _, hidden_dev, half = own.shape
    total = sum(r.shape[0] for r in rows)
    step = min(1024, half)
    lanes = whole_lanes(hidden_dev)
    weight = pl.BlockSpec((None, hidden_dev, step), lambda i: (0, 0, i))
    return pl.pallas_call(
        functools.partial(pull_kernel, len(rows)),
        grid=(half // step,),
        in_specs=[pl.BlockSpec((r.shape[0], step), lambda i: (0, i)) for r in rows] + [weight] * 2,
        out_specs=pl.BlockSpec((2, total, lanes), lambda i: (0, 0, 0)),
        out_shape=jax.ShapeDtypeStruct((2, total, lanes), F32),
        compiler_params=params(),
        cost_estimate=cost(),
        name="pull",
    )(*rows, own, other)


def sort_kernel(source, saved, out):
    count, _, total = saved.shape
    pick = (source[...] == lax.broadcasted_iota(jnp.int32, (source.shape[0], total), 1)).astype(BF16)
    for i in range(count):
        out[i] = lax.dot_general(pick, saved[i], TURN_RIGHT, preferred_element_type=F32).astype(BF16)


def sort_call(source, saved):
    count, hidden_dev, total = saved.shape
    block = total // RING
    return pl.pallas_call(
        sort_kernel,
        grid=(RING,),
        in_specs=[
            pl.BlockSpec((block, 1), lambda i: (i, 0)),
            pl.BlockSpec(saved.shape, lambda i: (0, 0, 0)),
        ],
        out_specs=pl.BlockSpec((count, block, hidden_dev), lambda i: (0, i, 0)),
        out_shape=jax.ShapeDtypeStruct((count, total, hidden_dev), BF16),
        compiler_params=params(),
        cost_estimate=cost(),
        name="sort",
    )(source, saved)


def slots_kernel(near, *refs):
    pulls, saved, weights = refs[:4], refs[4], refs[5:9]
    outs, (hidden_out, d_gate, d_up, score, value_ref) = refs[9 : 9 + PIECES], refs[9 + PIECES :]
    step = pl.program_id(0)
    piece, half = outs[0].shape
    hidden_dev = saved.shape[2]
    total, terms = None, []
    for d in range(2):
        near_pull = pulls[0][d] + pulls[1][1 - d]
        far_pull = pulls[2][d] + pulls[3][1 - d]
        pull = jnp.where(step < near, near_pull, far_pull)[:, :hidden_dev]
        pre_gate, pre_up = saved[2 * d].astype(F32), saved[2 * d + 1].astype(F32)
        sigmoid_gate = jax.nn.sigmoid(pre_gate)
        active = pre_gate * sigmoid_gate
        hidden = (active * pre_up).astype(BF16)
        hidden_out[d] = hidden
        point = jnp.sum(hidden.astype(F32) * pull, axis=1, keepdims=True)
        total = point if total is None else total + point
        slope = pre_up * (sigmoid_gate * (1.0 + pre_gate * (1.0 - sigmoid_gate)))
        gate_part = (pull * slope).astype(BF16)
        up_part = (pull * active).astype(BF16)
        d_gate[d] = gate_part
        d_up[d] = up_part
        terms += [(gate_part, weights[2 * d]), (up_part, weights[2 * d + 1])]
    score[...] = total
    run = min(512, half)
    for n in range(0, half, run):
        value = None
        for left, weight in terms:
            term = jnp.dot(left, weight[:, n : n + run], preferred_element_type=F32)
            value = term if value is None else value + term
        value_ref[:, n : n + run] = value.astype(BF16)

    def write(i):
        for j in range(2):
            outs[2 * i + j][...] = value_ref[j * piece : (j + 1) * piece, :]

    for i in range(RING):
        pl.when(step == i)(functools.partial(write, i))


def slots_call(pulls, saved, own, other):
    _, total, hidden_dev = saved.shape
    half = own.shape[2]
    block = total // RING
    near, lanes = pulls[0].shape[1] // block, pulls[0].shape[2]
    shape = jax.ShapeDtypeStruct
    near_spec = pl.BlockSpec((2, block, lanes), lambda i: (0, jnp.minimum(i, near - 1), 0))
    far_spec = pl.BlockSpec((2, block, lanes), lambda i: (0, jnp.maximum(i - near, 0), 0))
    units = pl.BlockSpec((2, block, hidden_dev), lambda i: (0, i, 0))
    four = pl.BlockSpec((4, block, hidden_dev), lambda i: (0, i, 0))
    gate = pl.BlockSpec((None, hidden_dev, half), lambda i: (1, 0, 0))
    up = pl.BlockSpec((None, hidden_dev, half), lambda i: (2, 0, 0))
    out = pl.pallas_call(
        functools.partial(slots_kernel, near),
        grid=(RING,),
        in_specs=[near_spec, near_spec, far_spec, far_spec, four, gate, up, gate, up],
        out_specs=[pl.BlockSpec((block // 2, half), lambda i: (0, 0))] * PIECES
        + [units, units, units, pl.BlockSpec((block, 1), lambda i: (i, 0))],
        out_shape=[shape((block // 2, half), BF16)] * PIECES
        + [shape((2, total, hidden_dev), BF16)] * 3
        + [shape((total, 1), F32)],
        scratch_shapes=[pltpu.VMEM((block, half), BF16)],
        compiler_params=params(),
        cost_estimate=cost(),
        name="slots",
    )(*pulls, saved, own, own, other, other)
    return out[:PIECES], *out[PIECES:]


def arrange_kernel(place, *refs):
    weights, outs = refs[:3], refs[3:]
    features = outs[0].shape[2]

    def copy(core):
        for d, out in enumerate(outs):
            first = (core + d) % 2 * features
            for i, weight in enumerate(weights):
                out[i] = weight[:, first : first + features]

    for core in range(2):
        pl.when(place[RING] == core)(functools.partial(copy, core))


def arrange_call(place, weights, features):
    hidden_dev, width = weights[0].shape
    shape = jax.ShapeDtypeStruct((3, hidden_dev, RING * features), BF16)
    block = (3, hidden_dev, features)
    return pl.pallas_call(
        arrange_kernel,
        grid_spec=pltpu.PrefetchScalarGridSpec(
            num_scalar_prefetch=1,
            grid=(RING,),
            in_specs=[pl.BlockSpec((hidden_dev, 2 * features), lambda r, t: (0, t[r]))] * 3,
            out_specs=[pl.BlockSpec(block, lambda r, t: (0, 0, r))] * 2,
        ),
        out_shape=[shape, shape],
        compiler_params=params(),
        cost_estimate=cost(),
        name="arrange",
    )(place, *weights)


def finish_kernel(place, factor, *refs):
    ins, outs = refs[:6], refs[6:]
    features = ins[0].shape[1]

    def write(core):
        for d in range(2):
            first = (core + d) % 2 * features
            for i, out in enumerate(outs):
                value = factor[0] * ins[2 * i + d][...].astype(F32)
                out[:, first : first + features] = value.astype(BF16)

    for core in range(2):
        pl.when(place[RING] == core)(functools.partial(write, core))


def finish_call(place, factor, pairs, features):
    hidden_dev, half = pairs[0][0].shape
    return pl.pallas_call(
        finish_kernel,
        grid_spec=pltpu.PrefetchScalarGridSpec(
            num_scalar_prefetch=1,
            grid=(RING,),
            in_specs=[pl.BlockSpec(memory_space=pltpu.SMEM)]
            + [pl.BlockSpec((hidden_dev, features), lambda r, t: (0, r))] * 6,
            out_specs=[pl.BlockSpec((None, hidden_dev, 2 * features), lambda r, t: (0, 0, t[r]))] * 3,
        ),
        out_shape=[jax.ShapeDtypeStruct((1, hidden_dev, 2 * half), BF16)] * 3,
        compiler_params=params(),
        cost_estimate=cost(),
        name="finish",
    )(place, factor, *[p for pair in pairs for p in pair])


def grads_kernel(row_count, left_count, gate_count, *refs):
    rows, refs = refs[:row_count], refs[row_count:]
    gates, refs = refs[:gate_count], refs[gate_count:]
    lefts, outs, square = refs[:left_count], refs[left_count : 3 * left_count], refs[3 * left_count]
    turned = refs[3 * left_count + 1]

    @pl.when(pl.program_id(0) == 0)
    def _():
        square[...] = jnp.zeros_like(square)
        for i, left in enumerate(lefts):
            for d in range(2):
                value = left[d].astype(F32)
                if gates:
                    value = value * jnp.concatenate([g[:, 0:1] for g in gates], axis=0).astype(F32)
                turned[2 * i + d] = value.T.astype(BF16)

    right = jnp.concatenate([r[...] for r in rows], axis=0)
    total = jnp.zeros((8, right.shape[1]), F32)
    for i, out in enumerate(outs):
        raw = jnp.dot(turned[i], right, preferred_element_type=F32)
        out[...] = raw.astype(BF16)
        total = total + jnp.sum((raw * raw).reshape(-1, 8, raw.shape[1]), axis=0)
    square[...] += total


def grads_call(rows, gates, lefts, half):
    _, total, hidden_dev = lefts[0].shape
    step = min(512, half)
    shape = jax.ShapeDtypeStruct
    in_specs = [pl.BlockSpec((r.shape[0], step), lambda j: (0, j)) for r in rows]
    in_specs += [pl.BlockSpec((g.shape[0], LANES), lambda j: (0, half // LANES)) for g in gates]
    in_specs += [pl.BlockSpec((2, total, hidden_dev), lambda j: (0, 0, 0))] * len(lefts)
    out = pl.pallas_call(
        functools.partial(grads_kernel, len(rows), len(lefts), len(gates)),
        grid=(half // step,),
        in_specs=in_specs,
        out_specs=[pl.BlockSpec((hidden_dev, step), lambda j: (0, j))] * (2 * len(lefts))
        + [pl.BlockSpec((8, step), lambda j: (0, 0))],
        out_shape=[shape((hidden_dev, half), BF16)] * (2 * len(lefts)) + [shape((8, step), F32)],
        scratch_shapes=[pltpu.VMEM((2 * len(lefts), hidden_dev, total), BF16)],
        compiler_params=params(),
        cost_estimate=cost(),
        name="grads",
    )(*rows, *gates, *lefts)
    return out[0:-1:2], out[1:-1:2], jnp.sum(out[-1])


def local(
    normed_input,
    output_grad,
    expert_ids,
    slot_pos,
    router_weight,
    gate_weight,
    up_weight,
    down_weight,
    saved_gate,
    saved_up,
):
    z, c, x, h, y = (lax.axis_index(name) for name in ("z", "c", "x", "h", "y"))
    width, experts = router_weight.shape
    tokens, features = normed_input.shape
    hidden_dev = gate_weight.shape[1]
    slot_total = saved_gate.shape[2]
    capacity = slot_total // (8 * RING)
    piece = RING * capacity
    block = 2 * piece
    half = RING * features

    near_expert = ((expert_ids % 2 + h) % 2) * RING + (expert_ids // 2 - x) % RING
    live_mask = slot_pos < capacity
    address = near_expert * capacity + slot_pos
    table = jnp.arange(block, dtype=jnp.int32)[None, :]
    first_pick = (address[:, 0:1] == table) & live_mask[:, 0:1]
    second_pick = (address[:, 1:2] == table) & live_mask[:, 1:2]
    pick_matrix = (first_pick | second_pick).astype(BF16)

    def place(matrix, values):
        return lax.dot_general(matrix, values, TURN_LEFT, preferred_element_type=F32).astype(BF16)

    def exchange_x(rows, sign):
        parts = rows.reshape(2, RING, capacity, -1)
        out = [parts[:, 0]] + [turn(parts[:, a], "x", sign * a) for a in range(1, RING)]
        return [jnp.concatenate([part[b] for part in out], axis=0) for b in range(2)]

    def gather_z(rows):
        return jnp.concatenate([rows] + [turn(rows, "z", r) for r in range(1, RING)], axis=1)

    def add(*terms):
        return functools.reduce(lambda a, b: a + b, [t.astype(F32) for t in terms])

    barrier = lax.optimization_barrier

    def spread_x(rows):
        parts = [rows[a * capacity : (a + 1) * capacity] for a in range(RING)]
        return jnp.concatenate(parts[:1] + [turn(parts[a], "x", a) for a in range(1, RING)], axis=0)

    dy_placed = place(pick_matrix, output_grad)
    near, far = dy_placed[:piece], dy_placed[piece:]
    far = swap(far, "h")
    near = spread_x(near)
    router_rows = lax.dynamic_slice_in_dim(router_weight, (z * 2 + c) * features, features, 0)
    logits = jnp.dot(normed_input, router_rows, preferred_element_type=F32)
    logits = sum_pair(after(logits, dy_placed), "c")
    sections = jnp.stack([(z - r) % RING for r in range(RING)] + [c]).astype(jnp.int32)
    weights = after((down_weight[0], gate_weight[0], up_weight[0]), dy_placed)
    own_weights, other_weights = arrange_call(sections, weights, features)
    near, far, logits, own_weights, other_weights = barrier((near, far, logits, own_weights, other_weights))

    near = gather_z(near)
    logits = sum_ring(logits, "z")
    far = spread_x(far)
    columns = jnp.arange(experts, dtype=jnp.int32)[None, :]
    first_hot = (columns == expert_ids[:, 0:1]).astype(F32)
    second_hot = (columns == expert_ids[:, 1:2]).astype(F32)
    pair_hot = first_hot - second_hot
    first_share = jax.nn.sigmoid(
        jnp.sum(logits * first_hot, axis=1) - jnp.sum(logits * second_hot, axis=1)
    )
    gate_first = first_share.astype(BF16).astype(F32)
    gate_second = (1.0 - first_share).astype(BF16).astype(F32)
    gate_matrix = jnp.where(first_pick, gate_first[:, None], 0.0) + jnp.where(
        second_pick, gate_second[:, None], 0.0
    )
    gated = jnp.concatenate([normed_input, jnp.ones((tokens, LANES), BF16)], axis=1)
    x_placed = place(gate_matrix.astype(BF16), gated)
    near, far, x_placed = barrier((near, far, x_placed))

    near_left, near_right = turn(near, "y", 1), turn(near, "y", -1)
    far = gather_z(far)
    x_near, x_far = exchange_x(x_placed, 1)
    other_weights = swap(after(other_weights, near), "c")
    saved = after(jnp.concatenate([saved_gate, saved_up], axis=0), near)
    saved = jnp.concatenate([saved, swap(saved, "c")], axis=0)
    far, x_near, x_far, saved, other_weights = barrier((far, x_near, x_far, saved, other_weights))

    far_left, far_right = turn(far, "y", 1), turn(far, "y", -1)
    x_far = swap(x_far, "h")
    x_near_z = gather_z(x_near[:, :features])
    order = jnp.arange(slot_total, dtype=jnp.int32)
    turn_y = order // block
    from_y = (y + jnp.where(turn_y < 2, turn_y, 5 - turn_y)) % RING
    from_h = (h + (order // piece) % 2) % 2
    from_x = (x - (order // capacity) % RING) % RING
    source = ((from_x * 2 + from_h) * RING + from_y) * capacity + order % capacity
    saved = sort_call(source[:, None], saved)
    near_left, near_right, x_far, x_near = barrier((near_left, near_right, x_far, x_near))
    near_across = turn(near_left, "y", 1)
    x_far_z = gather_z(x_far[:, :features])
    far_left, far_right, saved = barrier((far_left, far_right, saved))

    far_across = turn(far_right, "y", -1)
    dy_pieces = [near, far, near_right, far_right, near_left, far_left]
    near_pull = pull_call(dy_pieces, own_weights, other_weights)
    near_across, far_across, x_near_z, x_far_z = barrier((near_across, far_across, x_near_z, x_far_z))
    across = [near_across, far_across]
    x_rows = jnp.concatenate(
        [
            jnp.concatenate([x_near_z, x_near[:, features:]], axis=1),
            jnp.concatenate([x_far_z, x_far[:, features:]], axis=1),
        ],
        axis=0,
    )

    x_left, x_right = turn(x_rows, "y", 1), turn(x_rows, "y", -1)
    far_pull = pull_call(across, own_weights, other_weights)
    pulls = [near_pull, swap(near_pull, "c"), far_pull, swap(far_pull, "c")]
    dx, hidden, d_gate, d_up, score = slots_call(pulls, saved, own_weights, other_weights)

    from_left, from_right = turn(dx[6], "y", 1), turn(dx[7], "y", -1)
    score = score.reshape(RING, block)
    scores = [turn(score[1], "y", 1), turn(score[2], "y", -1), turn(score[3], "y", 2)]
    from_left, from_right, x_left, x_right = barrier((from_left, from_right, x_left, x_right))

    to_right = add(dx[2], from_left).astype(BF16)
    to_left = add(dx[5], from_right).astype(BF16)
    moved = [
        (turn(right, "y", 1), turn(left, "y", -1))
        for right, left in ((dx[3], to_left), (to_right, dx[4]))
    ]
    scores = after(scores, to_left, to_right)
    score = sum_ring(score[0] + scores[0] + scores[1] + scores[2], "z").reshape(2, RING, capacity)
    moved[0], score, x_left, x_right = barrier((moved[0], score, x_left, x_right))

    x_across = turn(x_left[:piece], "y", 1), turn(x_right[piece:], "y", -1)
    sums = [add(dx[1 - i], *pair).astype(BF16) for i, pair in enumerate(moved)]

    def turn_z(own):
        return [turn(own[:, r * features : (r + 1) * features], "z", -r) for r in range(1, RING)]

    parts = [turn_z(sums[0]), None]
    score = jnp.stack([score[0], swap(score[1], "h")])
    score = [score[:, 0]] + [turn(score[:, a], "x", -a) for a in range(1, RING)]
    score = jnp.stack(score, axis=1).reshape(1, block)
    parts[0], x_across, score = barrier((parts[0], x_across, score))
    far = add(sums[0][:, :features], *parts[0]).astype(BF16)
    x_pieces = [x_rows, x_right, x_left, *x_across]
    own_two, other_two, two_square = grads_call(x_pieces, [], [d_gate, d_up], half)
    sums[1], hidden = after((sums[1], hidden), two_square)
    parts[1] = turn_z(sums[1])
    (own_down,), (other_down,), down_square = grads_call(dy_pieces + across, x_pieces, [hidden], half)
    first_grad = jnp.sum(jnp.where(first_pick, score, 0.0), axis=1)
    second_grad = jnp.sum(jnp.where(second_pick, score, 0.0), axis=1)
    logit_step = (first_grad - second_grad) * first_share * (1.0 - first_share)
    logit_grad = pair_hot * logit_step[:, None]
    router_term = lax.dot_general(
        logit_grad, normed_input.astype(F32), TURN_LEFT, precision=lax.Precision.HIGHEST
    )
    parts[1], router_term, two_square, down_square = barrier(
        (parts[1], router_term, two_square, down_square)
    )
    near = add(sums[1][:, :features], *parts[1]).astype(BF16)

    far = swap(far, "h")
    message = jnp.concatenate(
        [router_term, jnp.full((8, features), down_square + two_square, F32)], axis=0
    )
    message = sum_turns(message, "y")
    far, message = barrier((far, message))
    back_dx = exchange_x(jnp.concatenate([near, far], axis=0), -1)
    message = sum_turns(message, "x")
    back_dx, message = barrier((back_dx, message))
    other_down = swap(other_down, "c")
    other_two = [swap(part, "c") for part in other_two]
    message = sum_pair(message, "h")
    raw_router = message[:experts]
    square_sum = jnp.full((8, LANES), message[experts, 0] + jnp.sum(raw_router * raw_router), F32)
    square_sum = sum_turns(sum_pair(square_sum, "c"), "z")[0, 0]
    row_count = features // (8 * RING)
    raw_router = lax.dynamic_slice_in_dim(
        raw_router, ((x * 2 + h) * RING + y) * row_count, row_count, 1
    ).T
    back_dx = jnp.concatenate(back_dx, axis=0)
    token_dx = jnp.dot(gate_matrix, back_dx.astype(F32), precision=lax.Precision.HIGHEST)
    input_grad = (
        token_dx
        + lax.dot_general(
            logit_grad, router_rows.astype(F32), TURN_RIGHT, precision=lax.Precision.HIGHEST
        )
    ).astype(BF16)
    entry_count = 3.0 * experts * hidden_dev * 8 * RING * width + 1.0 * width * experts
    factor = 1.0 / jnp.maximum(jnp.sqrt(square_sum / entry_count), 1.0)
    pairs = [(own_two[0], other_two[0]), (own_two[1], other_two[1]), (own_down, other_down)]
    grad_gate, grad_up, grad_down = finish_call(sections, factor.reshape(1), pairs, features)
    return (input_grad, factor * raw_router, grad_gate, grad_up, grad_down)


def solution(mesh):
    fine = Mesh(mesh.devices.reshape(4, 2, 4, 2, 4), ("z", "c", "x", "h", "y"))
    section, expert, edata = ("z", "c"), ("x", "h"), "y"
    rows = P((*expert, edata), section)
    ids = P((*expert, edata), None)
    weight = P(expert, (*section, edata), None)
    in_specs = (rows, rows, ids, ids, P(), weight, weight, weight, weight, weight)
    out_specs = (rows, P((*section, *expert, edata), None), weight, weight, weight)
    return jax.shard_map(local, mesh=fine, in_specs=in_specs, out_specs=out_specs, check_vma=False)
```

```python
import functools

import jax
import jax.numpy as jnp
from jax import lax
from jax.experimental import pallas as pl
from jax.experimental.pallas import tpu as pltpu
from jax.sharding import Mesh, PartitionSpec as P

F32 = jnp.float32
BF16 = jnp.bfloat16
RING = 4
PIECES = 8
LANES = 128
TURN_RIGHT = (((1,), (1,)), ((), ()))
TURN_LEFT = (((0,), (0,)), ((), ()))


def turn(value, axis, step):
    return lax.ppermute(value, axis, [(i, (i + step) % RING) for i in range(RING)])


def swap(value, axis):
    return lax.ppermute(value, axis, [(0, 1), (1, 0)])


def sum_ring(value, axis):
    for bit in (1, 2):
        value = value + lax.ppermute(value, axis, [(i, i ^ bit) for i in range(RING)])
    return value


def sum_turns(value, axis):
    one, two, three = turn(value, axis, 1), turn(value, axis, 2), turn(value, axis, 3)
    return (value + two) + (one + three)


def sum_pair(value, axis):
    return value + swap(value, axis)


def after(value, *others):
    return lax.optimization_barrier((value,) + others)[0]


def params():
    return pltpu.CompilerParams(vmem_limit_bytes=60 * 2**20)


def cost():
    return pl.CostEstimate(flops=1, bytes_accessed=1, transcendentals=0)


def whole_lanes(count):
    return -(-count // LANES) * LANES


def pull_kernel(count, *refs):
    rows, weights, out = refs[:count], refs[count : count + 2], refs[count + 2]
    hidden_dev = weights[0].shape[0]

    @pl.when(pl.program_id(0) == 0)
    def _():
        out[...] = jnp.zeros_like(out)

    left = jnp.concatenate([ref[...] for ref in rows], axis=0)
    for d, weight in enumerate(weights):
        out[d, :, :hidden_dev] += lax.dot_general(left, weight[...], TURN_RIGHT, preferred_element_type=F32)


def pull_call(rows, own, other):
    _, hidden_dev, half = own.shape
    total = sum(r.shape[0] for r in rows)
    step = min(1024, half)
    lanes = whole_lanes(hidden_dev)
    weight = pl.BlockSpec((None, hidden_dev, step), lambda i: (0, 0, i))
    return pl.pallas_call(
        functools.partial(pull_kernel, len(rows)),
        grid=(half // step,),
        in_specs=[pl.BlockSpec((r.shape[0], step), lambda i: (0, i)) for r in rows] + [weight] * 2,
        out_specs=pl.BlockSpec((2, total, lanes), lambda i: (0, 0, 0)),
        out_shape=jax.ShapeDtypeStruct((2, total, lanes), F32),
        compiler_params=params(),
        cost_estimate=cost(),
        name="pull",
    )(*rows, own, other)


def sort_kernel(source, saved, out):
    count, _, total = saved.shape
    pick = (source[...] == lax.broadcasted_iota(jnp.int32, (source.shape[0], total), 1)).astype(BF16)
    for i in range(count):
        out[i] = lax.dot_general(pick, saved[i], TURN_RIGHT, preferred_element_type=F32).astype(BF16)


def sort_call(source, saved):
    count, hidden_dev, total = saved.shape
    block = total // RING
    return pl.pallas_call(
        sort_kernel,
        grid=(RING,),
        in_specs=[
            pl.BlockSpec((block, 1), lambda i: (i, 0)),
            pl.BlockSpec(saved.shape, lambda i: (0, 0, 0)),
        ],
        out_specs=pl.BlockSpec((count, block, hidden_dev), lambda i: (0, i, 0)),
        out_shape=jax.ShapeDtypeStruct((count, total, hidden_dev), BF16),
        compiler_params=params(),
        cost_estimate=cost(),
        name="sort",
    )(source, saved)


def slots_kernel(near, *refs):
    pulls, saved, weights = refs[:4], refs[4], refs[5:9]
    outs, (hidden_out, d_gate, d_up, score, value_ref) = refs[9 : 9 + PIECES], refs[9 + PIECES :]
    step = pl.program_id(0)
    piece, half = outs[0].shape
    hidden_dev = saved.shape[2]
    total, terms = None, []
    for d in range(2):
        near_pull = pulls[0][d] + pulls[1][1 - d]
        far_pull = pulls[2][d] + pulls[3][1 - d]
        pull = jnp.where(step < near, near_pull, far_pull)[:, :hidden_dev]
        pre_gate, pre_up = saved[2 * d].astype(F32), saved[2 * d + 1].astype(F32)
        sigmoid_gate = jax.nn.sigmoid(pre_gate)
        active = pre_gate * sigmoid_gate
        hidden = (active * pre_up).astype(BF16)
        hidden_out[d] = hidden
        point = jnp.sum(hidden.astype(F32) * pull, axis=1, keepdims=True)
        total = point if total is None else total + point
        slope = pre_up * (sigmoid_gate * (1.0 + pre_gate * (1.0 - sigmoid_gate)))
        gate_part = (pull * slope).astype(BF16)
        up_part = (pull * active).astype(BF16)
        d_gate[d] = gate_part
        d_up[d] = up_part
        terms += [(gate_part, weights[2 * d]), (up_part, weights[2 * d + 1])]
    score[...] = total
    run = min(512, half)
    for n in range(0, half, run):
        value = None
        for left, weight in terms:
            term = jnp.dot(left, weight[:, n : n + run], preferred_element_type=F32)
            value = term if value is None else value + term
        value_ref[:, n : n + run] = value.astype(BF16)

    def write(i):
        for j in range(2):
            outs[2 * i + j][...] = value_ref[j * piece : (j + 1) * piece, :]

    for i in range(RING):
        pl.when(step == i)(functools.partial(write, i))


def slots_call(pulls, saved, own, other):
    _, total, hidden_dev = saved.shape
    half = own.shape[2]
    block = total // RING
    near, lanes = pulls[0].shape[1] // block, pulls[0].shape[2]
    shape = jax.ShapeDtypeStruct
    near_spec = pl.BlockSpec((2, block, lanes), lambda i: (0, jnp.minimum(i, near - 1), 0))
    far_spec = pl.BlockSpec((2, block, lanes), lambda i: (0, jnp.maximum(i - near, 0), 0))
    units = pl.BlockSpec((2, block, hidden_dev), lambda i: (0, i, 0))
    four = pl.BlockSpec((4, block, hidden_dev), lambda i: (0, i, 0))
    gate = pl.BlockSpec((None, hidden_dev, half), lambda i: (1, 0, 0))
    up = pl.BlockSpec((None, hidden_dev, half), lambda i: (2, 0, 0))
    out = pl.pallas_call(
        functools.partial(slots_kernel, near),
        grid=(RING,),
        in_specs=[near_spec, near_spec, far_spec, far_spec, four, gate, up, gate, up],
        out_specs=[pl.BlockSpec((block // 2, half), lambda i: (0, 0))] * PIECES
        + [units, units, units, pl.BlockSpec((block, 1), lambda i: (i, 0))],
        out_shape=[shape((block // 2, half), BF16)] * PIECES
        + [shape((2, total, hidden_dev), BF16)] * 3
        + [shape((total, 1), F32)],
        scratch_shapes=[pltpu.VMEM((block, half), BF16)],
        compiler_params=params(),
        cost_estimate=cost(),
        name="slots",
    )(*pulls, saved, own, own, other, other)
    return out[:PIECES], *out[PIECES:]


def arrange_kernel(place, *refs):
    weights, outs = refs[:3], refs[3:]
    features = outs[0].shape[2]

    def copy(core):
        for d, out in enumerate(outs):
            first = (core + d) % 2 * features
            for i, weight in enumerate(weights):
                out[i] = weight[:, first : first + features]

    for core in range(2):
        pl.when(place[RING] == core)(functools.partial(copy, core))


def arrange_call(place, weights, features):
    hidden_dev, width = weights[0].shape
    shape = jax.ShapeDtypeStruct((3, hidden_dev, RING * features), BF16)
    block = (3, hidden_dev, features)
    return pl.pallas_call(
        arrange_kernel,
        grid_spec=pltpu.PrefetchScalarGridSpec(
            num_scalar_prefetch=1,
            grid=(RING,),
            in_specs=[pl.BlockSpec((hidden_dev, 2 * features), lambda r, t: (0, t[r]))] * 3,
            out_specs=[pl.BlockSpec(block, lambda r, t: (0, 0, r))] * 2,
        ),
        out_shape=[shape, shape],
        compiler_params=params(),
        cost_estimate=cost(),
        name="arrange",
    )(place, *weights)


def finish_kernel(place, factor, *refs):
    ins, outs = refs[:6], refs[6:]
    features = ins[0].shape[1]

    def write(core):
        for d in range(2):
            first = (core + d) % 2 * features
            for i, out in enumerate(outs):
                value = factor[0] * ins[2 * i + d][...].astype(F32)
                out[:, first : first + features] = value.astype(BF16)

    for core in range(2):
        pl.when(place[RING] == core)(functools.partial(write, core))


def finish_call(place, factor, pairs, features):
    hidden_dev, half = pairs[0][0].shape
    return pl.pallas_call(
        finish_kernel,
        grid_spec=pltpu.PrefetchScalarGridSpec(
            num_scalar_prefetch=1,
            grid=(RING,),
            in_specs=[pl.BlockSpec(memory_space=pltpu.SMEM)]
            + [pl.BlockSpec((hidden_dev, features), lambda r, t: (0, r))] * 6,
            out_specs=[pl.BlockSpec((None, hidden_dev, 2 * features), lambda r, t: (0, 0, t[r]))] * 3,
        ),
        out_shape=[jax.ShapeDtypeStruct((1, hidden_dev, 2 * half), BF16)] * 3,
        compiler_params=params(),
        cost_estimate=cost(),
        name="finish",
    )(place, factor, *[p for pair in pairs for p in pair])


def grads_kernel(row_count, left_count, gate_count, *refs):
    rows, refs = refs[:row_count], refs[row_count:]
    gates, refs = refs[:gate_count], refs[gate_count:]
    lefts, outs, square = refs[:left_count], refs[left_count : 3 * left_count], refs[3 * left_count]
    turned = refs[3 * left_count + 1]

    @pl.when(pl.program_id(0) == 0)
    def _():
        square[...] = jnp.zeros_like(square)
        for i, left in enumerate(lefts):
            for d in range(2):
                value = left[d].astype(F32)
                if gates:
                    value = value * jnp.concatenate([g[:, 0:1] for g in gates], axis=0).astype(F32)
                turned[2 * i + d] = value.T.astype(BF16)

    right = jnp.concatenate([r[...] for r in rows], axis=0)
    total = jnp.zeros((8, right.shape[1]), F32)
    for i, out in enumerate(outs):
        raw = jnp.dot(turned[i], right, preferred_element_type=F32)
        out[...] = raw.astype(BF16)
        total = total + jnp.sum((raw * raw).reshape(-1, 8, raw.shape[1]), axis=0)
    square[...] += total


def grads_call(rows, gates, lefts, half):
    _, total, hidden_dev = lefts[0].shape
    step = half // RING
    shape = jax.ShapeDtypeStruct
    in_specs = [pl.BlockSpec((r.shape[0], step), lambda j: (0, j)) for r in rows]
    in_specs += [pl.BlockSpec((g.shape[0], LANES), lambda j: (0, half // LANES)) for g in gates]
    in_specs += [pl.BlockSpec((2, total, hidden_dev), lambda j: (0, 0, 0))] * len(lefts)
    out = pl.pallas_call(
        functools.partial(grads_kernel, len(rows), len(lefts), len(gates)),
        grid=(half // step,),
        in_specs=in_specs,
        out_specs=[pl.BlockSpec((hidden_dev, step), lambda j: (0, j))] * (2 * len(lefts))
        + [pl.BlockSpec((8, step), lambda j: (0, 0))],
        out_shape=[shape((hidden_dev, half), BF16)] * (2 * len(lefts)) + [shape((8, step), F32)],
        scratch_shapes=[pltpu.VMEM((2 * len(lefts), hidden_dev, total), BF16)],
        compiler_params=params(),
        cost_estimate=cost(),
        name="grads",
    )(*rows, *gates, *lefts)
    return out[0:-1:2], out[1:-1:2], out[-1]


def local(
    normed_input,
    output_grad,
    expert_ids,
    slot_pos,
    router_weight,
    gate_weight,
    up_weight,
    down_weight,
    saved_gate,
    saved_up,
):
    z, c, x, h, y = (lax.axis_index(name) for name in ("z", "c", "x", "h", "y"))
    width, experts = router_weight.shape
    tokens, features = normed_input.shape
    hidden_dev = gate_weight.shape[1]
    slot_total = saved_gate.shape[2]
    capacity = slot_total // (8 * RING)
    piece = RING * capacity
    block = 2 * piece
    half = RING * features

    near_expert = ((expert_ids % 2 + h) % 2) * RING + (expert_ids // 2 - x) % RING
    live_mask = slot_pos < capacity
    address = near_expert * capacity + slot_pos
    table = jnp.arange(block, dtype=jnp.int32)[None, :]
    first_pick = (address[:, 0:1] == table) & live_mask[:, 0:1]
    second_pick = (address[:, 1:2] == table) & live_mask[:, 1:2]
    pick_matrix = (first_pick | second_pick).astype(BF16)

    def place(matrix, values):
        return lax.dot_general(matrix, values, TURN_LEFT, preferred_element_type=F32).astype(BF16)

    def exchange_x(rows, sign):
        parts = rows.reshape(2, RING, capacity, -1)
        out = [parts[:, 0]] + [turn(parts[:, a], "x", sign * a) for a in range(1, RING)]
        return [jnp.concatenate([part[b] for part in out], axis=0) for b in range(2)]

    def gather_z(rows):
        return jnp.concatenate([rows] + [turn(rows, "z", r) for r in range(1, RING)], axis=1)

    def add(*terms):
        return functools.reduce(lambda a, b: a + b, [t.astype(F32) for t in terms])

    barrier = lax.optimization_barrier

    def spread_x(rows):
        parts = [rows[a * capacity : (a + 1) * capacity] for a in range(RING)]
        return jnp.concatenate(parts[:1] + [turn(parts[a], "x", a) for a in range(1, RING)], axis=0)

    dy_placed = place(pick_matrix, output_grad)
    near, far = dy_placed[:piece], dy_placed[piece:]
    far = swap(far, "h")
    near = spread_x(near)
    router_rows = lax.dynamic_slice_in_dim(router_weight, (z * 2 + c) * features, features, 0)
    logits = jnp.dot(normed_input, router_rows, preferred_element_type=F32)
    logits = sum_pair(after(logits, dy_placed), "c")
    sections = jnp.stack([(z - r) % RING for r in range(RING)] + [c]).astype(jnp.int32)
    weights = after((down_weight[0], gate_weight[0], up_weight[0]), dy_placed)
    own_weights, other_weights = arrange_call(sections, weights, features)
    near, far, logits, own_weights, other_weights = barrier((near, far, logits, own_weights, other_weights))

    near = gather_z(near)
    logits = sum_ring(logits, "z")
    far = spread_x(far)
    columns = jnp.arange(experts, dtype=jnp.int32)[None, :]
    first_hot = (columns == expert_ids[:, 0:1]).astype(F32)
    second_hot = (columns == expert_ids[:, 1:2]).astype(F32)
    pair_hot = first_hot - second_hot
    first_share = jax.nn.sigmoid(
        jnp.sum(logits * first_hot, axis=1) - jnp.sum(logits * second_hot, axis=1)
    )
    gate_first = first_share.astype(BF16).astype(F32)
    gate_second = (1.0 - first_share).astype(BF16).astype(F32)
    gate_matrix = jnp.where(first_pick, gate_first[:, None], 0.0) + jnp.where(
        second_pick, gate_second[:, None], 0.0
    )
    gated = jnp.concatenate([normed_input, jnp.ones((tokens, LANES), BF16)], axis=1)
    x_placed = place(gate_matrix.astype(BF16), gated)
    near, far, x_placed = barrier((near, far, x_placed))

    near_left, near_right = turn(near, "y", 1), turn(near, "y", -1)
    far = gather_z(far)
    x_near, x_far = exchange_x(x_placed, 1)
    other_weights = swap(after(other_weights, near), "c")
    saved = after(jnp.concatenate([saved_gate, saved_up], axis=0), near)
    saved = jnp.concatenate([saved, swap(saved, "c")], axis=0)
    far, x_near, x_far, saved, other_weights = barrier((far, x_near, x_far, saved, other_weights))

    far_left, far_right = turn(far, "y", 1), turn(far, "y", -1)
    x_far = swap(x_far, "h")
    x_near_z = gather_z(x_near[:, :features])
    order = jnp.arange(slot_total, dtype=jnp.int32)
    turn_y = order // block
    from_y = (y + jnp.where(turn_y < 2, turn_y, 5 - turn_y)) % RING
    from_h = (h + (order // piece) % 2) % 2
    from_x = (x - (order // capacity) % RING) % RING
    source = ((from_x * 2 + from_h) * RING + from_y) * capacity + order % capacity
    saved = sort_call(source[:, None], saved)
    near_left, near_right, x_far, x_near = barrier((near_left, near_right, x_far, x_near))
    near_across = turn(near_left, "y", 1)
    x_far_z = gather_z(x_far[:, :features])
    far_left, far_right, saved = barrier((far_left, far_right, saved))

    far_across = turn(far_right, "y", -1)
    dy_pieces = [near, far, near_right, far_right, near_left, far_left]
    near_pull = pull_call(dy_pieces, own_weights, other_weights)
    near_across, far_across, x_near_z, x_far_z = barrier((near_across, far_across, x_near_z, x_far_z))
    across = [near_across, far_across]
    x_rows = jnp.concatenate(
        [
            jnp.concatenate([x_near_z, x_near[:, features:]], axis=1),
            jnp.concatenate([x_far_z, x_far[:, features:]], axis=1),
        ],
        axis=0,
    )

    x_left, x_right = turn(x_rows, "y", 1), turn(x_rows, "y", -1)
    far_pull = pull_call(across, own_weights, other_weights)
    pulls = [near_pull, swap(near_pull, "c"), far_pull, swap(far_pull, "c")]
    dx, hidden, d_gate, d_up, score = slots_call(pulls, saved, own_weights, other_weights)

    from_left, from_right = turn(dx[6], "y", 1), turn(dx[7], "y", -1)
    score = score.reshape(RING, block)
    scores = [turn(score[1], "y", 1), turn(score[2], "y", -1), turn(score[3], "y", 2)]
    from_left, from_right, x_left, x_right = barrier((from_left, from_right, x_left, x_right))

    to_right = add(dx[2], from_left).astype(BF16)
    to_left = add(dx[5], from_right).astype(BF16)
    moved = [
        (turn(right, "y", 1), turn(left, "y", -1))
        for right, left in ((dx[3], to_left), (to_right, dx[4]))
    ]
    scores = after(scores, to_left, to_right)
    score = sum_ring(score[0] + scores[0] + scores[1] + scores[2], "z").reshape(2, RING, capacity)
    moved[0], score, x_left, x_right = barrier((moved[0], score, x_left, x_right))

    x_across = turn(x_left[:piece], "y", 1), turn(x_right[piece:], "y", -1)
    sums = [add(dx[1 - i], *pair).astype(BF16) for i, pair in enumerate(moved)]

    def turn_z(own):
        return [turn(own[:, r * features : (r + 1) * features], "z", -r) for r in range(1, RING)]

    parts = [turn_z(sums[0]), None]
    score = jnp.stack([score[0], swap(score[1], "h")])
    score = [score[:, 0]] + [turn(score[:, a], "x", -a) for a in range(1, RING)]
    score = jnp.stack(score, axis=1).reshape(1, block)
    parts[0], x_across, score = barrier((parts[0], x_across, score))
    far = add(sums[0][:, :features], *parts[0]).astype(BF16)
    x_pieces = [x_rows, x_right, x_left, *x_across]
    own_two, other_two, two_square = grads_call(x_pieces, [], [d_gate, d_up], half)
    sums[1], hidden = after((sums[1], hidden), two_square)
    parts[1] = turn_z(sums[1])
    (own_down,), (other_down,), down_square = grads_call(dy_pieces + across, x_pieces, [hidden], half)
    first_grad = jnp.sum(jnp.where(first_pick, score, 0.0), axis=1)
    second_grad = jnp.sum(jnp.where(second_pick, score, 0.0), axis=1)
    logit_step = (first_grad - second_grad) * first_share * (1.0 - first_share)
    logit_grad = pair_hot * logit_step[:, None]
    router_term = lax.dot_general(
        logit_grad, normed_input.astype(F32), TURN_LEFT, precision=lax.Precision.HIGHEST
    )
    parts[1], router_term, two_square, down_square = barrier(
        (parts[1], router_term, two_square, down_square)
    )
    near = add(sums[1][:, :features], *parts[1]).astype(BF16)

    far = swap(far, "h")
    message = jnp.concatenate([router_term, down_square + two_square], axis=0)
    message = sum_turns(message, "y")
    far, message = barrier((far, message))
    back_dx = exchange_x(jnp.concatenate([near, far], axis=0), -1)
    message = sum_turns(message, "x")
    back_dx, message = barrier((back_dx, message))
    other_down = swap(other_down, "c")
    other_two = [swap(part, "c") for part in other_two]
    message = sum_pair(message, "h")
    raw_router = message[:experts]
    square_sum = jnp.sum(raw_router * raw_router + message[experts:])
    square_sum = jnp.full((8, LANES), square_sum, F32)
    square_sum = sum_turns(sum_pair(square_sum, "c"), "z")[0, 0]
    row_count = features // (8 * RING)
    raw_router = lax.dynamic_slice_in_dim(
        raw_router, ((x * 2 + h) * RING + y) * row_count, row_count, 1
    ).T
    back_dx = jnp.concatenate(back_dx, axis=0)
    token_dx = jnp.dot(gate_matrix, back_dx.astype(F32), precision=lax.Precision.HIGHEST)
    input_grad = (
        token_dx
        + lax.dot_general(
            logit_grad, router_rows.astype(F32), TURN_RIGHT, precision=lax.Precision.HIGHEST
        )
    ).astype(BF16)
    entry_count = 3.0 * experts * hidden_dev * 8 * RING * width + 1.0 * width * experts
    factor = 1.0 / jnp.maximum(jnp.sqrt(square_sum / entry_count), 1.0)
    pairs = [(own_two[0], other_two[0]), (own_two[1], other_two[1]), (own_down, other_down)]
    grad_gate, grad_up, grad_down = finish_call(sections, factor.reshape(1), pairs, features)
    return (input_grad, factor * raw_router, grad_gate, grad_up, grad_down)


def solution(mesh):
    fine = Mesh(mesh.devices.reshape(4, 2, 4, 2, 4), ("z", "c", "x", "h", "y"))
    section, expert, edata = ("z", "c"), ("x", "h"), "y"
    rows = P((*expert, edata), section)
    ids = P((*expert, edata), None)
    weight = P(expert, (*section, edata), None)
    in_specs = (rows, rows, ids, ids, P(), weight, weight, weight, weight, weight)
    out_specs = (rows, P((*section, *expert, edata), None), weight, weight, weight)
    return jax.shard_map(local, mesh=fine, in_specs=in_specs, out_specs=out_specs, check_vma=False)
```
